256 devices in a mesh: blk: 128 (over x_lo, z, y, core), stretch: 2 (over x_hi).
Axes of the slice: x: 4 (x_hi: 2, x_lo: 2; x = x_hi * 2 + x_lo), y: 4, z: 8, core: 2. Of those that a mesh axis runs over, the one named last changes fastest.
Arguments:
- activations: bfloat16 [32768, 2048], P('blk', 'stretch'), may hold values from -6 to 6
- document_ids: int32 [32768], replicated, may hold values from 0 to 511, never falling along the last dimension, each value on 1 to 128 neighbouring positions
- joint_input_weights: bfloat16 [128, 2048, 1536], P('blk', 'stretch'), may hold values from -0.125 to 0.125
- output_weights: bfloat16 [128, 1024, 2048], P('blk', None, 'stretch'), may hold values from -0.1875 to 0.1875
- norm_gains: bfloat16 [128, 2048], P('blk', 'stretch'), may hold values from 0.5 to 1.5
Outputs:
- input_weight_grad: bfloat16 [128, 2048, 1536], P('blk', 'stretch')
- output_weight_grad: bfloat16 [128, 1024, 2048], P('blk', None, 'stretch')
The draws below stay inside these ranges and needn't reach their ends.
Inputs may be any that keep to these rules, and one draw needn't show every extreme that they name: `document_ids`: document numbers never fall along the tokens; a document spans at most half of 256 positions.
All inputs are finite; a program needn't handle non-finite values.
Results may differ from the reference program's by a relative error of at most 0.015.
Values may be sent and summed in bfloat16 or wider, within the bound.
No kernel may reach another device: no remote copies, remote signals or barrier semaphores. Data moves between devices by JAX's collectives and lax.ppermute only.
A program may use at most 128 MiB of HBM per device.

```python
import math
from functools import partial
import jax
import jax.numpy as jnp
import numpy as np
from jax import lax

MODEL_WIDTH = 2048
HEAD_WIDTH = 64
QUERY_HEADS = 16
KEY_VALUE_HEADS = 4
TOK_DEV = 256
CYCLE_LAYERS = 128
TOKENS = 32768
N_BLK = 128


def shard_levels(key, dims, pieces, low, top_value):
    loudness, own = 1.0, jax.random.fold_in(key, 6)
    for dim, parts in pieces:
        steps = jnp.exp(jax.random.uniform(jax.random.fold_in(own, dim), (parts,), jnp.float32, low / len(pieces), top_value / len(pieces)))
        loudness = loudness * jnp.repeat(steps, dims[dim] // parts).reshape([-1 if axis == dim else 1 for axis in range(len(dims))])
    return loudness


def split_up(number_of, total, reach, lean):
    loads = [(1 << 20) // math.isqrt(grade ** lean) + 1 for grade in range(2, number_of + 1)]
    rest, counts = total - reach - (number_of - 1), [1] * (number_of - 1)
    while rest > 0:
        movable = [i for i in range(number_of - 1) if counts[i] < reach]
        pool, budget = sum([loads[i] for i in movable]), rest
        for i in movable:
            extra = min(reach - counts[i], max(1, budget * loads[i] // pool), rest)
            counts[i] = counts[i] + extra
            rest = rest - extra
    return np.array([reach] + counts)


def ragged(key, count, total, limit, skew):
    if count == 2:
        one = jax.random.randint(key, (), max(1, total - limit), min(limit, total - 1) + 1)
        return jnp.stack([one, total - one])
    tallies = jnp.asarray(split_up(count, total, limit, skew), jnp.int32)
    pairs = (count - 1) // 2
    source_of, receiver = tallies[1:1 + 2 * pairs:2], tallies[2:2 + 2 * pairs:2]
    margin = jnp.minimum(source_of - 1, limit - receiver)
    passed = jax.random.randint(jax.random.fold_in(key, 1), (pairs,), 0, 1 << 20) % (margin + 1)
    tallies = tallies.at[1:1 + 2 * pairs:2].set(source_of - passed).at[2:2 + 2 * pairs:2].set(receiver + passed)
    return tallies[jax.random.permutation(jax.random.fold_in(key, 2), count)]


def gaussian(stream_key, dims, deviation, bound, split=(), kind=jnp.bfloat16):
    drawn = deviation * jax.random.normal(stream_key, dims, jnp.float32)
    if split:
        drawn = drawn * shard_levels(stream_key, dims, split, -0.22, 0.18)
    return jnp.clip(drawn, -bound, bound).astype(kind)


def setup_inputs(seed: int = 0) -> dict:
    splits = jax.random.split(jax.random.key(seed), 6)
    activations = gaussian(splits[0], (TOKENS, MODEL_WIDTH), 1.0, 6.0, ((0, 128), (1, 2)))
    document_ids = jnp.searchsorted(jnp.cumsum(ragged(splits[1], 4 * N_BLK, TOKENS, TOK_DEV // 2, 2)), jnp.arange(TOKENS), side="right").astype(jnp.int32)
    joint_input_weights = gaussian(splits[2], (CYCLE_LAYERS, MODEL_WIDTH, (QUERY_HEADS + 2 * KEY_VALUE_HEADS) * HEAD_WIDTH), MODEL_WIDTH ** -0.5, 0.125, ((0, 128), (1, 2)))
    output_weights = gaussian(splits[3], (CYCLE_LAYERS, QUERY_HEADS * HEAD_WIDTH, MODEL_WIDTH), (QUERY_HEADS * HEAD_WIDTH) ** -0.5, 0.1875, ((0, 128), (2, 2)))
    norm_gains = jnp.clip(1.0 + 0.1 * jax.random.normal(splits[4], (CYCLE_LAYERS, MODEL_WIDTH), jnp.float32), 0.5, 1.5).astype(jnp.bfloat16)
    return {"activations": activations, "document_ids": document_ids, "joint_input_weights": joint_input_weights, "output_weights": output_weights, "norm_gains": norm_gains}


EPS = 1e-05
THETA = 10000.0
PRECISE = lax.Precision.HIGHEST

def rotate(matrix, cosine, sine_part):
    half_size = matrix.shape[-1] // 2
    first_half = matrix[..., :half_size]
    second = matrix[..., half_size:]
    return jnp.concatenate([first_half * cosine - second * sine_part, first_half * sine_part + second * cosine], axis=-1)

def attend(projected_input, doc_ids):
    count_of_rows = projected_input.shape[0]
    half_size = HEAD_WIDTH // 2
    queries_per_group = QUERY_HEADS // KEY_VALUE_HEADS
    position = jnp.arange(count_of_rows, dtype=jnp.float32)[:, None]
    frequency = THETA ** (-2.0 * jnp.arange(half_size, dtype=jnp.float32) / HEAD_WIDTH)
    angles = position * frequency[None, :]
    cosine = jnp.cos(angles)
    sine_part = jnp.sin(angles)
    query_rows = projected_input[:, :QUERY_HEADS * HEAD_WIDTH].reshape(count_of_rows, KEY_VALUE_HEADS, queries_per_group, HEAD_WIDTH)
    query_rows = rotate(query_rows, cosine[:, None, None, :], sine_part[:, None, None, :])
    key_rows_rotated = projected_input[:, QUERY_HEADS * HEAD_WIDTH:(QUERY_HEADS + KEY_VALUE_HEADS) * HEAD_WIDTH].reshape(count_of_rows, KEY_VALUE_HEADS, HEAD_WIDTH)
    key_rows_rotated = rotate(key_rows_rotated, cosine[:, None, :], sine_part[:, None, :])
    value_rows = projected_input[:, (QUERY_HEADS + KEY_VALUE_HEADS) * HEAD_WIDTH:].reshape(count_of_rows, KEY_VALUE_HEADS, HEAD_WIDTH)
    row_index = jnp.arange(count_of_rows)[:, None]
    col_index = jnp.arange(count_of_rows)[None, :]
    allowed = (col_index <= row_index) & (doc_ids[:, None] == doc_ids[None, :])

    def one_group(operands):
        group_queries, group_keys, group_values = operands
        scores = jnp.einsum('tgd,sd->gts', group_queries, group_keys, precision=PRECISE) * HEAD_WIDTH ** (-0.5)
        scores = jnp.where(allowed[None], scores, -1e+30)
        row_max = lax.optimization_barrier(jnp.max(scores, axis=2, keepdims=True))
        weights = jnp.exp(scores - row_max)
        weights = weights / lax.optimization_barrier(jnp.sum(weights, axis=2, keepdims=True))
        return jnp.einsum('gts,sd->tgd', weights, group_values, precision=PRECISE)
    results = lax.map(one_group, (jnp.moveaxis(query_rows, 1, 0), jnp.moveaxis(key_rows_rotated, 1, 0), jnp.moveaxis(value_rows, 1, 0)))
    return jnp.moveaxis(results, 0, 1).reshape(count_of_rows, QUERY_HEADS * HEAD_WIDTH)

def layer_forward(inputs, layer, doc_ids):
    joint_input_weights, output_weights, norm_gains = layer
    inputs_float = inputs.astype(jnp.float32)
    scale_one = lax.rsqrt(lax.optimization_barrier(jnp.sum(inputs_float * inputs_float, axis=1, keepdims=True)) / MODEL_WIDTH + EPS)
    normed_one = (inputs_float * scale_one * norm_gains.astype(jnp.float32)).astype(jnp.bfloat16)
    projected_input = jnp.dot(normed_one, joint_input_weights, preferred_element_type=jnp.float32)
    attended = attend(projected_input, doc_ids).astype(jnp.bfloat16)
    result = (inputs_float + jnp.dot(attended, output_weights, preferred_element_type=jnp.float32)).astype(jnp.bfloat16)
    stored = (inputs_float, scale_one, normed_one, projected_input, attended)
    return (result, stored)

def layer_backward(upstream, layer, stored, doc_ids):
    joint_input_weights, output_weights, norm_gains = layer
    inputs_float, scale_one, normed_one, projected_input, attended = stored
    upstream_bf = upstream.astype(jnp.bfloat16)
    attended_grad = jnp.dot(upstream_bf, output_weights.T, preferred_element_type=jnp.float32)
    out_grad = jnp.dot(attended.T, upstream_bf, preferred_element_type=jnp.float32)
    projected_grad = jax.vjp(partial(attend, doc_ids=doc_ids), projected_input)[1](attended_grad)[0].astype(jnp.bfloat16)
    attn_grad = jnp.dot(normed_one.T, projected_grad, preferred_element_type=jnp.float32)
    normed_one_grad = jnp.dot(projected_grad, joint_input_weights.T, preferred_element_type=jnp.float32)
    scaled_one = norm_gains.astype(jnp.float32) * normed_one_grad
    input_sum = lax.optimization_barrier(jnp.sum(scaled_one * inputs_float, axis=1, keepdims=True))
    input_grad = upstream + scale_one * scaled_one - inputs_float * scale_one ** 3 * input_sum / MODEL_WIDTH
    return (input_grad, (attn_grad, out_grad))

def microbatch(batches, doc_batches, joint_input_weights, output_weights, norm_gains, position):
    previous = (position + N_BLK - 1) % N_BLK
    own_layer = (joint_input_weights[position], output_weights[position], norm_gains[position])
    prior_layer = (joint_input_weights[previous], output_weights[previous], norm_gains[previous])
    doc_ids = doc_batches[position]
    first_out, first_stored = layer_forward(batches[position], own_layer, doc_ids)
    second_out, second_stored = layer_forward(first_out, prior_layer, doc_ids)
    upstream, prior_grads = layer_backward(second_out.astype(jnp.float32), prior_layer, second_stored, doc_ids)
    unused_grad, own_grads = layer_backward(upstream, own_layer, first_stored, doc_ids)
    return (own_grads, prior_grads)

def reference(activations, document_ids, joint_input_weights, output_weights, norm_gains):
    batches = activations.reshape(N_BLK, TOK_DEV, MODEL_WIDTH)
    doc_batches = document_ids.reshape(N_BLK, TOK_DEV)
    process = partial(microbatch, batches, doc_batches, joint_input_weights, output_weights, norm_gains)
    first_own, first_prior = process(jnp.int32(0))

    def advance(held_grads, position):
        own_grads, prior_grads = process(position)
        summed_in = (held_grads[0] + prior_grads[0]).astype(jnp.bfloat16)
        summed_out = (held_grads[1] + prior_grads[1]).astype(jnp.bfloat16)
        return (own_grads, (summed_in, summed_out))
    last_own, stacked = lax.scan(advance, first_own, jnp.arange(1, N_BLK, dtype=jnp.int32))
    final_in = (last_own[0] + first_prior[0]).astype(jnp.bfloat16)[None]
    final_out = (last_own[1] + first_prior[1]).astype(jnp.bfloat16)[None]
    return (jnp.concatenate([stacked[0], final_in], axis=0), jnp.concatenate([stacked[1], final_out], axis=0))
```

```python
from functools import partial

import numpy as np
import jax
import jax.numpy as jnp
from jax import lax
from jax.experimental import pallas as pl
from jax.experimental.pallas import tpu as pltpu
from jax.sharding import PartitionSpec as P

MODEL_WIDTH = 2048
HEAD_WIDTH = 64
EPS = 1e-05
THETA = 10000.0
F32, BF16 = jnp.float32, jnp.bfloat16

T = 256
HALF = 1024
QW, KW = 512, 128
OWN = QW + 2 * KW
MSG = T + 16

NN = (((1,), (0,)), ((), ()))
NT = (((1,), (1,)), ((), ()))
TN = (((0,), (0,)), ((), ()))


def dot(left, right, dims=NN):
    return lax.dot_general(left, right, dims, preferred_element_type=F32)


def tables():
    lane = np.arange(128)
    angles = np.arange(T)[:, None] * THETA ** (-2.0 * (lane % 32) / HEAD_WIDTH)[None, :]
    sign = np.where(lane % 64 < 32, -1.0, 1.0)[None, :]
    return np.cos(angles).astype(np.float32), (np.sin(angles) * sign).astype(np.float32)


def lane_index(shape):
    return lax.broadcasted_iota(jnp.int32, shape, 1)


def exchange_halves(block):
    first = lane_index(block.shape) % 64 < 32
    return jnp.where(first, pltpu.roll(block, 96, 1), pltpu.roll(block, 32, 1))


def rotate(block, cosine, sine):
    return block * cosine + exchange_halves(block) * sine


def rotate_back(block, cosine, sine):
    return block * cosine - exchange_halves(block) * sine


def to_row(column):
    return jnp.transpose(jnp.broadcast_to(column, (T, 128)))[0:1, :]


def to_lanes(row):
    return jnp.transpose(jnp.broadcast_to(row, (128, T)))


def split_row(row):
    high = row.astype(BF16)
    low = (row - high.astype(F32)).astype(BF16)
    return high, low


def wide(tile, width):
    return jnp.concatenate([tile] * (width // 128), axis=1)


def put_sums(msg_ref, row):
    high, low = split_row(row)
    index = lax.broadcasted_iota(jnp.int32, (16, T), 0)
    rows = jnp.where(index == 0, high.astype(F32), jnp.where(index == 1, low.astype(F32), 0.0))
    msg_ref[T:, :T] = rows.astype(BF16)
    msg_ref[T:, T:] = jnp.zeros((16, OWN - T), BF16)


def get_sums(msg_ref):
    rows = msg_ref[T:, :T].astype(F32)
    return rows[0:1, :] + rows[1:2, :]


def gained(x_ref, gain_ref):
    return (x_ref[...].astype(F32) * gain_ref[...].astype(F32)).astype(BF16)


def send_projection_kernel(s_ref, x_ref, gain_ref, wq_ref, wk_ref, wv_ref, msg_ref, sums_ref):
    x = x_ref[...].astype(F32)
    normed = (x * gain_ref[...].astype(F32)).astype(BF16)
    msg_ref[:T, :QW] = dot(normed, wq_ref[...]).astype(BF16)
    both = jnp.concatenate([wk_ref[...], wv_ref[...]], axis=1)
    msg_ref[:T, QW:] = dot(normed, both).astype(BF16)
    row = to_row(jnp.sum(x * x, axis=1, keepdims=True))
    sums_ref[...] = jnp.broadcast_to(row, (8, T))
    put_sums(msg_ref, row)


def own_projection_kernel(s_ref, x_ref, gain_ref, wq_ref, wk_ref, wv_ref, out_ref):
    normed = gained(x_ref, gain_ref)
    out_ref[:, :QW] = dot(normed, wq_ref[...])
    both = jnp.concatenate([wk_ref[...], wv_ref[...]], axis=1)
    out_ref[:, QW:] = dot(normed, both)


def group_pair(block, group):
    low = lane_index(block.shape) < 64
    if group == 0:
        first = jnp.where(low, block, 0.0)
        return jnp.concatenate([first, pltpu.roll(first, 64, 1)], axis=0)
    second = jnp.where(low, 0.0, block)
    return jnp.concatenate([pltpu.roll(second, 64, 1), second], axis=0)


def attend_kernel(
    msg_ref, own_ref, sums_ref, drow_ref, dcol_ref, cos_ref, sin_ref,
    att_ref, q_ref, k_ref, v_ref, p_ref, scale_ref,
):
    sums = sums_ref[0:1, :] + get_sums(msg_ref)
    scale = to_lanes(lax.rsqrt(sums / MODEL_WIDTH + EPS))
    scale_ref[...] = scale
    cosine, sine = cos_ref[...], sin_ref[...]

    def column(start):
        cols = slice(start, start + 128)
        return (own_ref[:, cols] + msg_ref[:T, cols].astype(F32)) * scale

    k = rotate(column(QW), cosine, sine)
    v = column(QW + KW)
    k_ref[...] = k.astype(BF16)
    v_ref[...] = v.astype(BF16)
    key = lax.broadcasted_iota(jnp.int32, (T, T), 0)
    query = lax.broadcasted_iota(jnp.int32, (T, T), 1)
    bias = jnp.where((key <= query) & (dcol_ref[...] == drow_ref[...]), 0.0, -1e30)
    for group in range(2):
        keys = group_pair(k, group).astype(BF16)
        values = jnp.transpose(group_pair(v, group)).astype(BF16)
        outs = []
        for pair in (2 * group, 2 * group + 1):
            q = (rotate(column(128 * pair), cosine, sine) * 0.125).astype(BF16)
            q_ref[:, 128 * pair : 128 * pair + 128] = q
            scores = dot(keys, q, NT)
            for half in range(2):
                part = scores[T * half : T * half + T] + bias
                weights = jnp.exp(part - jnp.max(part, axis=0, keepdims=True))
                weights = weights * (1.0 / jnp.sum(weights, axis=0, keepdims=True))
                start = (2 * pair + half) * T
                p_ref[start : start + T, :] = weights.astype(BF16)
            outs.append(dot(values, p_ref[2 * pair * T : 2 * pair * T + 2 * T, :]))
        att_ref[:, T * group : T * group + T] = jnp.transpose(
            jnp.concatenate(outs, axis=0)
        ).astype(BF16)


def attend_back_kernel(
    with_sums, recv_ref, own_ref, q_ref, k_ref, v_ref, p_ref, cos_ref, sin_ref, pg_ref
):
    cosine, sine = cos_ref[...], sin_ref[...]
    k, v = k_ref[...].astype(F32), v_ref[...].astype(F32)
    low = lane_index((T, 128)) < 64
    total = jnp.zeros((T, 128), F32)
    dks, dvs = [], []
    for group in range(2):
        keys = jnp.transpose(group_pair(k, group)).astype(BF16)
        values = group_pair(v, group).astype(BF16)
        dk = jnp.zeros((T, 128), F32)
        dv = jnp.zeros((T, 128), F32)
        dqs = []
        for pair in (2 * group, 2 * group + 1):
            cols = slice(128 * pair, 128 * pair + 128)
            grad = own_ref[:, cols] + recv_ref[:, cols].astype(F32)
            q = q_ref[:, cols].astype(F32)
            dp = dot(values, grad.astype(BF16), NT)
            dss = []
            for half in range(2):
                start = (2 * pair + half) * T
                weights = p_ref[start : start + T, :]
                wide_weights = weights.astype(F32)
                part = dp[T * half : T * half + T]
                product = wide_weights * part
                ds = product - wide_weights * jnp.sum(product, axis=0, keepdims=True)
                ds = ds.astype(BF16)
                keep = low if half == 0 else jnp.logical_not(low)
                dv = dv + dot(weights, jnp.where(keep, grad, 0.0).astype(BF16))
                dk = dk + dot(ds, jnp.where(keep, q, 0.0).astype(BF16))
                dss.append(ds)
            dqs.append(dot(keys, jnp.concatenate(dss, axis=0)))
        dq = jnp.transpose(jnp.concatenate(dqs, axis=0))
        for i, pair in enumerate((2 * group, 2 * group + 1)):
            cols = slice(128 * pair, 128 * pair + 128)
            block = dq[:, 128 * i : 128 * i + 128]
            if with_sums:
                total = total + block * q_ref[:, cols].astype(F32)
            pg_ref[:T, cols] = rotate_back(block * 0.125, cosine, sine).astype(BF16)
        dks.append(dk + pltpu.roll(dk, 64, 1))
        dvs.append(dv + pltpu.roll(dv, 64, 1))
    dk = jnp.where(low, dks[0], dks[1])
    dv = jnp.where(low, dvs[0], dvs[1])
    pg_ref[:T, QW : QW + KW] = rotate_back(dk, cosine, sine).astype(BF16)
    pg_ref[:T, QW + KW :] = dv.astype(BF16)
    if with_sums:
        total = total + dk * k + dv * v
        put_sums(pg_ref, to_row(jnp.sum(total, axis=1, keepdims=True)))


def own_output_kernel(s_ref, x_ref, gain_ref, scale_ref, att_ref, w_ref, acc_ref, normed_ref):
    x = x_ref[...].astype(F32)
    acc_ref[...] = x + dot(att_ref[...], w_ref[...])
    scale = wide(scale_ref[...], HALF)
    normed_ref[...] = (x * scale * gain_ref[...].astype(F32)).astype(BF16)


def output_kernel(s_ref, acc_ref, att_ref, w_ref, out_ref):
    out_ref[...] = (acc_ref[...] + dot(att_ref[...], w_ref[...])).astype(BF16)


def output_turn_kernel(s_ref, acc_ref, att_ref, w_ref, out_ref, msg_ref):
    out = (acc_ref[...] + dot(att_ref[...], w_ref[...])).astype(BF16)
    out_ref[...] = out
    msg_ref[...] = dot(out, w_ref[...], NT).astype(BF16)


def output_back_kernel(s_ref, up_ref, w_ref, out_ref):
    out_ref[...] = dot(up_ref[...], w_ref[...], NT).astype(out_ref.dtype)


def own_back_kernel(s_ref, pg_ref, wq_ref, wk_ref, wv_ref, out_ref):
    both = jnp.concatenate([wk_ref[...], wv_ref[...]], axis=1)
    out_ref[...] = dot(pg_ref[:T, :QW], wq_ref[...], NT) + dot(pg_ref[:T, QW:], both, NT)


def input_back_kernel(
    s_ref, acc_ref, recv_ref, pg_ref, wq_ref, wk_ref, wv_ref, x_ref, gain_ref, scale_ref, up_ref,
    out_ref,
):
    both = jnp.concatenate([wk_ref[...], wv_ref[...]], axis=1)
    grad = acc_ref[...] + dot(recv_ref[:T, :QW], wq_ref[...], NT)
    grad = grad + dot(recv_ref[:T, QW:], both, NT)
    scale = scale_ref[...]
    sums = to_lanes((get_sums(recv_ref) + get_sums(pg_ref)) / MODEL_WIDTH)
    factor = wide(scale * scale * sums, HALF)
    out = up_ref[...].astype(F32) + wide(scale, HALF) * (gain_ref[...].astype(F32) * grad)
    out_ref[...] = (out - x_ref[...].astype(F32) * factor).astype(BF16)


def output_weight_kernel(s_ref, a1_ref, r1_ref, u1_ref, a2_ref, r2_ref, u2_ref, out_ref):
    s = s_ref[0]
    u1, u2 = u1_ref[...], u2_ref[...]
    out_ref[pl.ds(QW * s, QW), :] = (dot(a1_ref[...], u1, TN) + dot(a2_ref[...], u2, TN)).astype(BF16)
    out_ref[pl.ds(QW * (1 - s), QW), :] = (
        dot(r1_ref[...], u1, TN) + dot(r2_ref[...], u2, TN)
    ).astype(BF16)


def input_weight_kernel(own, s_ref, n1_ref, p1_ref, n2_ref, p2_ref, *rest):
    out_ref, held, sems = rest[-3:]
    owner = s_ref[0] if own else 1 - s_ref[0]
    n1, n2 = n1_ref[...], n2_ref[...]
    copies = []
    for i, (start, size, place) in enumerate(
        ((0, QW, QW * owner), (QW, KW, 1024 + KW * owner), (QW + KW, KW, 1280 + KW * owner))
    ):
        cols = slice(start, start + size)
        part = dot(n1, p1_ref[:T, cols], TN) + dot(n2, p2_ref[:T, cols], TN)
        held[:, cols] = part.astype(BF16)
        copy = pltpu.make_async_copy(
            held.at[:, cols], out_ref.at[:, pl.ds(pl.multiple_of(place, 128), size)], sems.at[i]
        )
        copy.start()
        copies.append(copy)
    for copy in copies:
        copy.wait()


PARAMS = pltpu.CompilerParams(vmem_limit_bytes=40 * 1024 * 1024)


def full(*shape):
    return pl.BlockSpec(shape, lambda i, s: (0,) * len(shape))


def weight_specs(own):
    def at(base):
        return lambda i, s: (0, base + (s[0] if own else 1 - s[0]))

    return [
        pl.BlockSpec((HALF, QW), at(0)),
        pl.BlockSpec((HALF, KW), at(8)),
        pl.BlockSpec((HALF, KW), at(10)),
    ]


def out_weight_spec(own):
    return pl.BlockSpec((QW, HALF), lambda i, s: (s[0] if own else 1 - s[0], 0))


def shape_of(dtype, *shape):
    return jax.ShapeDtypeStruct(shape, dtype)


def call(kernel, s, in_specs, outs, args, flops, name, out_specs=None, scratch=(), aliases=None):
    moved = sum(int(np.prod(a.shape)) * a.dtype.itemsize for a in list(args) + list(outs))
    return pl.pallas_call(
        kernel,
        grid_spec=pltpu.PrefetchScalarGridSpec(
            num_scalar_prefetch=1,
            grid=(1,),
            in_specs=in_specs,
            out_specs=out_specs or [full(*o.shape) for o in outs],
            scratch_shapes=list(scratch),
        ),
        out_shape=list(outs),
        compiler_params=PARAMS,
        cost_estimate=pl.CostEstimate(flops=flops, bytes_accessed=moved, transcendentals=0),
        input_output_aliases=aliases or {},
        name=name,
    )(s, *args)


def swap(value):
    return lax.ppermute(value, "stretch", [(0, 1), (1, 0)])


def hop(value, step):
    count = lax.axis_size("blk")
    return lax.ppermute(value, "blk", [(i, (i + step) % count) for i in range(count)])


def no_scalar(kernel):
    return lambda s_ref, *refs: kernel(*refs)


def forward_start(s, x, layer, docs, trig):
    w_in, w_out, gain = layer
    xw = [full(T, HALF), full(1, HALF)]
    msg, sums = call(
        send_projection_kernel, s, xw + weight_specs(False),
        [shape_of(BF16, MSG, OWN), shape_of(F32, 8, T)],
        [x, gain, w_in, w_in, w_in], 2 * T * HALF * OWN, "send_projection",
    )
    recv = swap(msg)
    (own,) = call(
        own_projection_kernel, s, xw + weight_specs(True), [shape_of(F32, T, OWN)],
        [x, gain, w_in, w_in, w_in], 2 * T * HALF * OWN, "own_projection",
    )
    att, q, k, v, p, scale = call(
        no_scalar(attend_kernel), s,
        [full(MSG, OWN), full(T, OWN), full(8, T), full(1, T), full(T, 1), full(T, 128), full(T, 128)],
        [
            shape_of(BF16, T, QW), shape_of(BF16, T, QW), shape_of(BF16, T, KW),
            shape_of(BF16, T, KW), shape_of(BF16, 8 * T, T), shape_of(F32, T, 128),
        ],
        [recv, own, sums, docs[None, :], docs[:, None], *trig], 2 * 8 * T * T * 512, "attend",
    )
    att_recv = swap(att)
    acc, normed = call(
        own_output_kernel, s,
        [full(T, HALF), full(1, HALF), full(T, 128), full(T, QW), out_weight_spec(True)],
        [shape_of(F32, T, HALF), shape_of(BF16, T, HALF)],
        [x, gain, scale, att, w_out], 2 * T * HALF * QW, "own_output",
    )
    return acc, normed, att, att_recv, (q, k, v, p), scale


def backward_start(s, recv, own, kept, trig, with_sums):
    q, k, v, p = kept
    (pg,) = call(
        no_scalar(partial(attend_back_kernel, with_sums)), s,
        [
            full(T, QW), full(T, QW), full(T, QW), full(T, KW), full(T, KW), full(8 * T, T),
            full(T, 128), full(T, 128),
        ],
        [shape_of(BF16, MSG if with_sums else T, OWN)],
        [recv, own, q, k, v, p, *trig], 2 * 8 * T * T * 1024, "attend_back",
    )
    return pg, swap(pg)


def output_back(s, up, w_out, own):
    (out,) = call(
        output_back_kernel, s, [full(T, HALF), out_weight_spec(own)],
        [shape_of(F32 if own else BF16, T, QW)], [up, w_out], 2 * T * HALF * QW, "output_back",
    )
    return out


def input_weights(s, own, n1, p1, n2, p2, held=None):
    specs = [full(*a.shape) for a in (n1, p1, n2, p2)]
    args = [n1, p1, n2, p2]
    if held is not None:
        specs.append(pl.BlockSpec(memory_space=pl.ANY))
        args.append(held)
    (out,) = call(
        partial(input_weight_kernel, own), s, specs, [shape_of(BF16, HALF, 1536)], args,
        2 * 2 * T * HALF * OWN, "input_weights",
        out_specs=[pl.BlockSpec(memory_space=pl.ANY)],
        scratch=[pltpu.VMEM((HALF, OWN), BF16), pltpu.SemaphoreType.DMA((3,))],
        aliases={5: 0} if held is not None else None,
    )
    return out


def shards(activations, document_ids, joint_input_weights, output_weights, norm_gains):
    blk = lax.axis_index("blk")
    s = lax.axis_index("stretch").astype(jnp.int32)[None]
    own_docs = lax.dynamic_slice_in_dim(document_ids, blk * T, T)
    next_blk = lax.rem(blk + 1, lax.axis_size("blk"))
    next_docs = lax.dynamic_slice_in_dim(document_ids, next_blk * T, T)
    w_in, w_out, gain = layer = (joint_input_weights[0], output_weights[0], norm_gains)
    trig = tuple(jnp.asarray(t) for t in tables())

    acc1, n1, a1, r1, kept1, _ = forward_start(s, activations, layer, own_docs, trig)
    (first_out,) = call(
        output_kernel, s, [full(T, HALF), full(T, QW), out_weight_spec(False)],
        [shape_of(BF16, T, HALF)], [acc1, r1, w_out], 2 * T * HALF * QW, "output",
    )

    x2 = hop(first_out, -1)
    acc2, n2, a2, r2, kept2, scale2 = forward_start(s, x2, layer, next_docs, trig)
    second_out, msg = call(
        output_turn_kernel, s, [full(T, HALF), full(T, QW), out_weight_spec(False)],
        [shape_of(BF16, T, HALF), shape_of(BF16, T, QW)], [acc2, r2, w_out],
        4 * T * HALF * QW, "output_turn",
    )
    recv = swap(msg)
    own = output_back(s, second_out, w_out, True)
    p2, p2_recv = backward_start(s, recv, own, kept2, trig, True)
    (acc,) = call(
        own_back_kernel, s, [full(MSG, OWN)] + weight_specs(True), [shape_of(F32, T, HALF)],
        [p2, w_in, w_in, w_in], 2 * T * HALF * OWN, "own_back",
    )
    (up2,) = call(
        input_back_kernel, s,
        [full(T, HALF), full(MSG, OWN), full(MSG, OWN)] + weight_specs(False)
        + [full(T, HALF), full(1, HALF), full(T, 128), full(T, HALF)],
        [shape_of(BF16, T, HALF)],
        [acc, p2_recv, p2, w_in, w_in, w_in, x2, gain, scale2, second_out],
        2 * T * HALF * OWN, "input_back",
    )

    up1 = hop(up2, 1)
    recv = swap(output_back(s, up1, w_out, False))
    own = output_back(s, up1, w_out, True)
    p1, p1_recv = backward_start(s, recv, own, kept1, trig, False)
    (total_out,) = call(
        output_weight_kernel, s,
        [full(T, QW), full(T, QW), full(T, HALF)] * 2, [shape_of(BF16, HALF, HALF)],
        [a1, r1, up1, a2, r2, second_out], 2 * 2 * T * HALF * HALF, "output_weights",
    )
    half_in = input_weights(s, True, n1, p1, n2, p2)
    total_in = input_weights(s, False, n1, p1_recv, n2, p2_recv, half_in)
    return (total_in[None], total_out[None])


def solution(mesh):
    placed = (
        P("blk", "stretch"),
        P(),
        P("blk", "stretch", None),
        P("blk", None, "stretch"),
        P("blk", "stretch"),
    )
    return jax.shard_map(
        shards,
        mesh=mesh,
        in_specs=placed,
        out_specs=(P("blk", "stretch", None), P("blk", None, "stretch")),
        check_vma=False,
    )
```

```python
from functools import partial

import numpy as np
import jax
import jax.numpy as jnp
from jax import lax
from jax.experimental import pallas as pl
from jax.experimental.pallas import tpu as pltpu
from jax.sharding import PartitionSpec as P

MODEL_WIDTH = 2048
HEAD_WIDTH = 64
EPS = 1e-05
THETA = 10000.0
F32, BF16 = jnp.float32, jnp.bfloat16

T = 256
R = 128
HALF = 1024
HEADS = 1024
KEYS = 256
JOINT = HEADS + 2 * KEYS
LOG2E = 1.4426950408889634

NN = (((1,), (0,)), ((), ()))
NT = (((1,), (1,)), ((), ()))
TN = (((0,), (0,)), ((), ()))


def dot(left, right, dims=NN):
    return lax.dot_general(left, right, dims, preferred_element_type=F32)


def tables():
    lane = np.arange(128)
    angles = np.arange(T)[:, None] * THETA ** (-2.0 * (lane % 32) / HEAD_WIDTH)[None, :]
    sign = np.where(lane % 64 < 32, -1.0, 1.0)[None, :]
    return np.cos(angles).astype(np.float32), (np.sin(angles) * sign).astype(np.float32)


def lane_index(shape):
    return lax.broadcasted_iota(jnp.int32, shape, 1)


def exchange_halves(block):
    first = lane_index(block.shape) % 64 < 32
    return jnp.where(first, pltpu.roll(block, 96, 1), pltpu.roll(block, 32, 1))


def rotate(block, cosine, sine):
    return block * cosine + exchange_halves(block) * sine


def rotate_back(block, cosine, sine):
    return block * cosine - exchange_halves(block) * sine


def wide(tile, width):
    return jnp.concatenate([tile] * (width // 128), axis=1)


def columns(index):
    return slice(128 * index, 128 * index + 128)


def project_kernel(x_ref, gain_ref, w_ref, msg_ref, own_ref, sums_ref):
    x = x_ref[...].astype(F32)
    normed = (x * gain_ref[...].astype(F32)).astype(BF16)
    own = dot(normed, w_ref[...])
    own_ref[...] = own
    msg_ref[:, :JOINT] = own.astype(BF16)
    sums = jnp.broadcast_to(jnp.sum(x * x, axis=1, keepdims=True), (R, 128))
    sums_ref[...] = sums
    high = sums.astype(BF16).astype(F32)
    lane = lane_index((R, 128))
    parts = jnp.where(lane == 0, high, jnp.where(lane == 1, sums - high, 0.0))
    msg_ref[:, JOINT:] = parts.astype(BF16)


def prepare_kernel(docs1_ref, docs2_ref, cos_in, sin_in, bias1_ref, bias2_ref, cos_ref, sin_ref):
    cos_ref[...] = cos_in[...]
    sin_ref[...] = sin_in[...]
    key = lax.broadcasted_iota(jnp.int32, (T, T), 0)
    query = lax.broadcasted_iota(jnp.int32, (T, T), 1)
    for docs_ref, bias_ref in ((docs1_ref, bias1_ref), (docs2_ref, bias2_ref)):
        of_query = jnp.broadcast_to(docs_ref[...], (T, T))
        same = jnp.transpose(of_query) == of_query
        bias_ref[...] = jnp.where((key <= query) & same, 0.0, -1e30)


def group_pair(block, half):
    low = lane_index(block.shape) < 64
    if half == 0:
        first = jnp.where(low, block, 0.0)
        return jnp.concatenate([first, pltpu.roll(first, 64, 1)], axis=0)
    second = jnp.where(low, 0.0, block)
    return jnp.concatenate([pltpu.roll(second, 64, 1), second], axis=0)


def group_pair_back(turned, half):
    part = turned[64 * half : 64 * half + 64]
    zero = jnp.zeros_like(part)
    return jnp.concatenate(
        [jnp.concatenate([part, zero], axis=1), jnp.concatenate([zero, part], axis=1)], axis=0
    )


def stack_pairs(blocks, group):
    return jnp.concatenate([blocks[2 * group], blocks[2 * group + 1]], axis=0)


def attend_kernel(stream, turn, msg_ref, own_ref, sums_ref, x_ref, w_ref, bias_ref, *rest):
    cos_ref, sin_ref = rest[:2]
    before = rest[2 : 2 + 2 * stream]
    outs = rest[2 + 2 * stream :]
    out_ref, att_ref, q_ref, k_ref, v_ref, p_ref, scale_ref = outs[:7]
    seen = R * (stream + 1)
    received = jnp.sum(msg_ref[:, JOINT:].astype(F32), axis=1, keepdims=True)
    scale = lax.rsqrt((sums_ref[...] + received) / MODEL_WIDTH + EPS)
    scale_ref[...] = scale
    cosine, sine = cos_ref[...], sin_ref[...]

    def column(index):
        cols = columns(index)
        return (own_ref[:, cols] + msg_ref[:, cols].astype(F32)) * scale

    ks = [rotate(column(8 + i), cosine, sine) for i in range(2)]
    vs = [column(10 + i) for i in range(2)]
    for i in range(2):
        k_ref[:, columns(i)] = ks[i].astype(BF16)
        v_ref[:, columns(i)] = vs[i].astype(BF16)
        if stream:
            ks[i] = jnp.concatenate([before[0][:, columns(i)].astype(F32), ks[i]], axis=0)
            vs[i] = jnp.concatenate([before[1][:, columns(i)].astype(F32), vs[i]], axis=0)
    qs = []
    for i in range(8):
        q = (rotate(column(i), cosine, sine) * (0.125 * LOG2E)).astype(BF16)
        q_ref[:, columns(i)] = q
        qs.append(q)
    bias = wide(bias_ref[...], T)
    scores = [
        dot(group_pair(ks[g // 2], g % 2).astype(BF16), stack_pairs(qs, g), NT) for g in range(4)
    ]
    turned = [jnp.transpose(v).astype(BF16) for v in vs]
    for g in range(4):
        ps = []
        for half in range(2):
            part = scores[g][seen * half : seen * half + seen] + bias
            weights = jnp.exp2(part - jnp.max(part, axis=0, keepdims=True))
            weights = weights * (1.0 / jnp.sum(weights, axis=0, keepdims=True))
            ps.append(weights.astype(BF16))
            start = (2 * g + half) * seen
            p_ref[start : start + seen, :] = ps[-1]
        out = dot(group_pair_back(turned[g // 2], g % 2), jnp.concatenate(ps, axis=0))
        out = jnp.transpose(out).astype(BF16)
        att_ref[:, columns(2 * g)] = out[:R]
        att_ref[:, columns(2 * g + 1)] = out[R:]
    out = (x_ref[...].astype(F32) + dot(att_ref[...], w_ref[...])).astype(BF16)
    out_ref[...] = out
    if turn:
        own = dot(out, w_ref[...], NT)
        outs[7][...] = own.astype(BF16)
        outs[8][...] = own


def attend_back(stream, with_sums, recv_ref, own_ref, q_ref, p_ref, cos_ref, sin_ref, kv, partial_refs, pg_ref):
    seen = R * (stream + 1)
    cosine, sine = cos_ref[...], sin_ref[...]
    ks, vs = [], []
    for i in range(2):
        cols = columns(i)
        ks.append(jnp.concatenate([r[:, cols] for r in kv[0::2]], axis=0).astype(F32))
        vs.append(jnp.concatenate([r[:, cols] for r in kv[1::2]], axis=0).astype(F32))
    grads = [own_ref[:, columns(i)] + recv_ref[:, columns(i)].astype(F32) for i in range(8)]
    low = lane_index((T, 128)) < 64
    dps = [
        dot(group_pair(vs[g // 2], g % 2).astype(BF16), stack_pairs(grads, g).astype(BF16), NT)
        for g in range(4)
    ]
    turned = [jnp.transpose(k).astype(BF16) for k in ks]
    total = jnp.zeros((R, 128), F32)
    dks, dvs = [], []
    for g in range(4):
        dss, ps = [], []
        for half in range(2):
            start = (2 * g + half) * seen
            weights = p_ref[start : start + seen, :]
            wide_weights = weights.astype(F32)
            product = wide_weights * dps[g][seen * half : seen * half + seen]
            ds = product - wide_weights * jnp.sum(product, axis=0, keepdims=True)
            dss.append(ds.astype(BF16))
            ps.append(weights)
        q = jnp.concatenate([q_ref[:, columns(2 * g)], q_ref[:, columns(2 * g + 1)]], axis=0)
        q = q.astype(F32)
        grad = stack_pairs(grads, g)
        sides = []
        for value in (q, grad):
            first = jnp.where(low, value, 0.0).astype(BF16)
            second = jnp.where(low, 0.0, value).astype(BF16)
            sides.append(jnp.concatenate([first, second], axis=0))
        dk = dot(jnp.concatenate(dss, axis=1), sides[0])
        dv = dot(jnp.concatenate(ps, axis=1), sides[1])
        dks.append(dk + pltpu.roll(dk, 64, 1))
        dvs.append(dv + pltpu.roll(dv, 64, 1))
        dq = jnp.transpose(dot(group_pair_back(turned[g // 2], g % 2), jnp.concatenate(dss, axis=0)))
        if with_sums:
            product = dq * q
            total = total + product[:R] + product[R:]
        for i in range(2):
            block = dq[R * i : R * i + R] * 0.125
            pg_ref[:, columns(2 * g + i)] = rotate_back(block, cosine, sine).astype(BF16)
    total = total * (1.0 / LOG2E)
    low = lane_index((seen, 128)) < 64
    for i in range(2):
        dk = jnp.where(low, dks[2 * i], dks[2 * i + 1]) * (1.0 / LOG2E)
        dv = jnp.where(low, dvs[2 * i], dvs[2 * i + 1])
        cols = columns(i)
        if stream:
            partial_refs[0][:, cols], partial_refs[1][:, cols] = dk[:R], dv[:R]
            dk, dv = dk[R:], dv[R:]
        else:
            dk, dv = dk + partial_refs[0][:, cols], dv + partial_refs[1][:, cols]
        if with_sums:
            total = total + dk * ks[i][-R:] + dv * vs[i][-R:]
        pg_ref[:, columns(8 + i)] = rotate_back(dk, cosine, sine).astype(BF16)
        pg_ref[:, columns(10 + i)] = dv.astype(BF16)
    return total


def attend_back_kernel(stream, with_input, *refs):
    count = 2 * (stream + 1)
    fixed, kv, rest = refs[:6], refs[6 : 6 + count], list(refs[6 + count :])
    if not stream:
        partials, rest = rest[:2], rest[2:]
    if with_input:
        (w_ref, x_ref, gain_ref, scale_ref, up_ref), rest = rest[:5], rest[5:]
    pg_ref, rest = rest[0], rest[1:]
    if stream:
        partials, rest = rest[:2], rest[2:]
    total = attend_back(stream, with_input, *fixed, kv, partials, pg_ref)
    if with_input:
        (out_ref,) = rest
        sums = jnp.sum(total, axis=1, keepdims=True) / MODEL_WIDTH
        grad = dot(pg_ref[...], w_ref[...], NT)
        scale = scale_ref[...]
        out = up_ref[...].astype(F32) + wide(scale, HALF) * (gain_ref[...].astype(F32) * grad)
        factor = wide(scale * scale * sums, HALF)
        out_ref[...] = (out - x_ref[...].astype(F32) * factor).astype(BF16)


def output_back_kernel(up_ref, w_ref, msg_ref, own_ref):
    own = dot(up_ref[...], w_ref[...], NT)
    msg_ref[...] = own.astype(BF16)
    own_ref[...] = own


def output_weight_kernel(*refs):
    att = jnp.concatenate([r[...] for r in refs[:4]], axis=0)
    up = jnp.concatenate([r[...] for r in refs[4:8]], axis=0)
    refs[8][...] = dot(att, up, TN).astype(BF16)


def input_weight_kernel(last, xa_ref, xb_ref, sa_ref, sb_ref, gain_ref, pa_ref, pb_ref, *rest):
    gain = gain_ref[...].astype(F32)
    normed = jnp.concatenate(
        [
            (x[...].astype(F32) * wide(s[...], x.shape[1]) * gain).astype(BF16)
            for x, s in ((xa_ref, sa_ref), (xb_ref, sb_ref))
        ],
        axis=0,
    )
    out = dot(normed, jnp.concatenate([pa_ref[...], pb_ref[...]], axis=0), TN)
    if last:
        out = out + rest[0][...]
    rest[-1][...] = out.astype(rest[-1].dtype)


PARAMS = pltpu.CompilerParams(vmem_limit_bytes=32 * 1024 * 1024)


def shape_of(dtype, *shape):
    return jax.ShapeDtypeStruct(shape, dtype)


def block(*shape, at=None):
    return pl.BlockSpec(shape, lambda i: at or (0,) * len(shape))


def call(kernel, args, outs, flops, name, specs=None, out_specs=None, grid=1):
    moved = sum(int(np.prod(a.shape)) * a.dtype.itemsize for a in list(args) + list(outs))
    specs = specs or {}
    return pl.pallas_call(
        kernel,
        grid=(grid,),
        in_specs=[specs.get(i) or block(*a.shape) for i, a in enumerate(args)],
        out_specs=out_specs or [block(*o.shape) for o in outs],
        out_shape=list(outs),
        compiler_params=PARAMS,
        cost_estimate=pl.CostEstimate(flops=flops, bytes_accessed=moved, transcendentals=0),
        name=name,
    )(*args)


def swap(value):
    return lax.ppermute(value, "stretch", [(0, 1), (1, 0)])


def hop(value, step):
    count = lax.axis_size("blk")
    return lax.ppermute(value, "blk", [(i, (i + step) % count) for i in range(count)])


IN_FLOPS = 2 * R * HALF * JOINT
OUT_FLOPS = 2 * R * HALF * HEADS


def after(value, *others):
    return lax.optimization_barrier((value, *others))[0]


def project(x, layer, spec=None):
    w_in, _, gain = layer
    return call(
        project_kernel, [x, gain, w_in],
        [shape_of(BF16, R, JOINT + 128), shape_of(F32, R, JOINT), shape_of(F32, R, 128)],
        IN_FLOPS, "project", specs={0: spec} if spec else None,
    )


def attend(stream, turn, x, parts, layer, bias, trig, before, spec=None):
    recv, own, sums = parts
    seen = R * (stream + 1)
    shapes = [
        shape_of(BF16, R, HALF), shape_of(BF16, R, HEADS), shape_of(BF16, R, HEADS),
        shape_of(BF16, R, KEYS), shape_of(BF16, R, KEYS), shape_of(BF16, 8 * seen, T),
        shape_of(F32, R, 128),
    ]
    if turn:
        shapes += [shape_of(BF16, R, HEADS), shape_of(F32, R, HEADS)]
    at = (stream, 0)
    specs = {
        5: block(seen, R, at=(0, stream)), 6: block(R, 128, at=at), 7: block(R, 128, at=at),
    }
    if spec:
        specs[3] = spec
    outs = call(
        partial(attend_kernel, stream, turn),
        [recv, own, sums, x, layer[1], bias, *trig, *before], shapes,
        OUT_FLOPS * (1 + turn) + 4 * 16 * R * seen * 128, "attend", specs=specs,
    )
    out, att, q, k, v, p, scale = outs[:7]
    kept = dict(x=x, att=att, q=q, kv=[k, v], p=p, scale=scale, out=out)
    if turn:
        kept["msg"], kept["own"] = outs[7:]
    return kept


def back(stream, recv, own, kept, trig, kv, partials, layer=None):
    seen = R * (stream + 1)
    args = [recv, own, kept["q"], kept["p"], *trig, *kv]
    if not stream:
        args += partials
    shapes = [shape_of(BF16, R, JOINT)]
    if stream:
        shapes += [shape_of(F32, R, KEYS)] * 2
    if layer:
        args += [layer[0], kept["x"], layer[2], kept["scale"], kept["out"]]
        shapes.append(shape_of(BF16, R, HALF))
    at = block(R, 128, at=(stream, 0))
    return call(
        partial(attend_back_kernel, stream, layer is not None), args, shapes,
        8 * 16 * R * seen * 128 + (IN_FLOPS if layer else 0), "attend_back",
        specs={4: at, 5: at},
    )


def output_back(up, layer):
    return call(
        output_back_kernel, [up, layer[1]], [shape_of(BF16, R, HEADS), shape_of(F32, R, HEADS)],
        OUT_FLOPS, "output_back",
    )


def input_weights(xs, scales, gain, pgs, acc, spec_of=None):
    parts = 4
    cut = HALF // parts
    rows = pl.BlockSpec((R, cut), lambda i: (0, i))
    out = pl.BlockSpec((cut, JOINT), lambda i: (i, 0))
    specs = {0: rows, 1: rows, 4: pl.BlockSpec((1, cut), lambda i: (0, i))}
    if spec_of:
        specs[0], specs[1] = spec_of(cut)
    args = [*xs, *scales, gain, *pgs]
    if acc is not None:
        specs[7] = out
        args.append(acc)
    return call(
        partial(input_weight_kernel, acc is not None), args,
        [shape_of(F32 if acc is None else BF16, HALF, JOINT)], 2 * IN_FLOPS, "input_weights",
        specs=specs, out_specs=[out], grid=parts,
    )[0]


def shards(activations, document_ids, joint_input_weights, output_weights, norm_gains):
    blk = lax.axis_index("blk")
    w_in, w_out, gain = layer = (joint_input_weights[0], output_weights[0], norm_gains)
    tables_in = [jnp.asarray(t) for t in tables()]

    rows = [block(R, HALF, at=(i, 0)) for i in range(2)]
    msg_a, own_a, sums_a = project(activations, layer, rows[0])
    recv_a = swap(msg_a)
    msg_b, own_b, sums_b = project(after(activations, msg_a), layer, rows[1])
    recv_b = swap(msg_b)
    ids = after(document_ids, msg_b)
    next_blk = lax.rem(blk + 1, lax.axis_size("blk"))
    docs = [
        lax.dynamic_slice_in_dim(ids, i * T, T).astype(F32)[None, :] for i in (blk, next_blk)
    ]
    bias1, bias2, *trig = call(
        prepare_kernel, [*docs, *tables_in],
        [shape_of(F32, T, T)] * 2 + [shape_of(F32, T, 128)] * 2, 4 * T * T, "prepare",
    )
    a1 = attend(0, False, activations, (recv_a, own_a, sums_a), layer, bias1, trig, [], rows[0])
    xa = hop(a1["out"], -1)
    b1 = attend(
        1, False, activations, (recv_b, own_b, sums_b), layer, bias1, trig, a1["kv"], rows[1]
    )
    xb = hop(b1["out"], -1)

    msg_a, own_a, sums_a = project(xa, layer)
    recv_a = swap(msg_a)
    msg_b, own_b, sums_b = project(after(xb, msg_a), layer)
    recv_b = swap(msg_b)
    a2 = attend(0, True, xa, (recv_a, own_a, sums_a), layer, bias2, trig, [])
    recv_a = swap(a2["msg"])
    b2 = attend(1, True, xb, (recv_b, own_b, sums_b), layer, bias2, trig, a2["kv"])
    recv_b = swap(b2["msg"])
    pgb2, dka, dva, up = back(1, recv_b, b2["own"], b2, trig, a2["kv"] + b2["kv"], None, layer)
    upb = hop(up, 1)
    pga2, up = back(0, recv_a, a2["own"], a2, trig, a2["kv"], [dka, dva], layer)
    upa = hop(up, 1)

    msg_b, own_b = output_back(upb, layer)
    recv_b = swap(msg_b)
    msg_a, own_a = output_back(after(upa, msg_b), layer)
    recv_a = swap(msg_a)
    acc = input_weights([xa, xb], [a2["scale"], b2["scale"]], gain, [pga2, pgb2], None)
    (total_out,) = call(
        output_weight_kernel,
        [k["att"] for k in (a1, b1, a2, b2)] + [upa, upb, a2["out"], b2["out"]],
        [shape_of(BF16, HEADS, HALF)], 4 * OUT_FLOPS, "output_weights",
    )
    pgb1, dka, dva = back(1, recv_b, own_b, b1, trig, a1["kv"] + b1["kv"], None)
    (pga1,) = back(0, recv_a, own_a, a1, trig, a1["kv"], [dka, dva])
    total_in = input_weights(
        [activations, activations], [a1["scale"], b1["scale"]], gain, [pga1, pgb1], acc,
        lambda cut: [pl.BlockSpec((R, cut), lambda i, r=r: (r, i)) for r in range(2)],
    )
    return (total_in[None], total_out[None])


def solution(mesh):
    placed = (
        P("blk", "stretch"),
        P(),
        P("blk", "stretch", None),
        P("blk", None, "stretch"),
        P("blk", "stretch"),
    )
    return jax.shard_map(
        shards,
        mesh=mesh,
        in_specs=placed,
        out_specs=(P("blk", "stretch", None), P("blk", None, "stretch")),
        check_vma=False,
    )
```

```python
from functools import partial

import numpy as np
import jax
import jax.numpy as jnp
from jax import lax
from jax.experimental import pallas as pl
from jax.experimental.pallas import tpu as pltpu
from jax.sharding import PartitionSpec as P

MODEL_WIDTH = 2048
HEAD_WIDTH = 64
EPS = 1e-05
THETA = 10000.0
F32, BF16 = jnp.float32, jnp.bfloat16

T = 256
R = 128
HALF = 1024
HEADS = 1024
KEYS = 256
JOINT = HEADS + 2 * KEYS
LOG2E = 1.4426950408889634

NN = (((1,), (0,)), ((), ()))
NT = (((1,), (1,)), ((), ()))
TN = (((0,), (0,)), ((), ()))


def dot(left, right, dims=NN):
    return lax.dot_general(left, right, dims, preferred_element_type=F32)


def tables():
    lane = np.arange(128)
    angles = np.arange(T)[:, None] * THETA ** (-2.0 * (lane % 32) / HEAD_WIDTH)[None, :]
    sign = np.where(lane % 64 < 32, -1.0, 1.0)[None, :]
    return np.cos(angles).astype(np.float32), (np.sin(angles) * sign).astype(np.float32)


def lane_index(shape):
    return lax.broadcasted_iota(jnp.int32, shape, 1)


def exchange_halves(block):
    first = lane_index(block.shape) % 64 < 32
    return jnp.where(first, pltpu.roll(block, 96, 1), pltpu.roll(block, 32, 1))


def rotate(block, cosine, sine):
    return block * cosine + exchange_halves(block) * sine


def rotate_back(block, cosine, sine):
    return block * cosine - exchange_halves(block) * sine


def wide(tile, width):
    return jnp.concatenate([tile] * (width // 128), axis=1)


def columns(index):
    return slice(128 * index, 128 * index + 128)


def project_first_kernel(x_in, gain_ref, w_in, *rest):
    outs, (x_ref, w_ref, held, x_sem, w_sems) = rest[:2], rest[2:]
    pieces = w_sems.shape[0]
    size = HALF // pieces
    copies = [pltpu.make_async_copy(x_in, x_ref, x_sem)]
    for i in range(pieces):
        rows = pl.ds(i * size, size)
        copies.append(pltpu.make_async_copy(w_in.at[rows], w_ref.at[rows], w_sems.at[i]))
    for copy in copies:
        copy.start()
    copies[0].wait()
    x = x_ref[...].astype(F32)
    normed = (x * gain_ref[...].astype(F32)).astype(BF16)
    for stream in range(2):
        put_sums(x[R * stream : R * stream + R], outs[stream])
    for i in range(pieces):
        copies[1 + i].wait()
        part = dot(normed[:, i * size : i * size + size], w_ref[i * size : i * size + size, :])
        if i:
            part = held[...] + part
        if i < pieces - 1:
            held[...] = part
    for stream in range(2):
        outs[stream][:, :JOINT] = part[R * stream : R * stream + R].astype(BF16)


def project_own_kernel(x_ref, gain_ref, w_ref, w_out_ref, *rest):
    outs, w_t_ref, w_out_t_ref = rest[:4], rest[4], rest[5]
    x = x_ref[...].astype(F32)
    own = dot((x * gain_ref[...].astype(F32)).astype(BF16), w_ref[...])
    for stream in range(2):
        rows = slice(R * stream, R * stream + R)
        outs[2 * stream][...] = own[rows]
        outs[2 * stream + 1][...] = token_sums(x[rows])
    w_t_ref[...] = jnp.transpose(w_ref[...])
    w_out_t_ref[...] = jnp.transpose(w_out_ref[...])


def project_kernel(x_ref, gain_ref, w_ref, *outs):
    x = x_ref[...].astype(F32)
    normed = (x * gain_ref[...].astype(F32)).astype(BF16)
    put_projection(x, dot(normed, w_ref[...]), *outs)


def token_sums(x):
    return jnp.broadcast_to(jnp.sum(x * x, axis=1, keepdims=True), (R, 128))


def put_sums(x, msg_ref):
    sums = token_sums(x)
    high = sums.astype(BF16).astype(F32)
    lane = lane_index((R, 128))
    parts = jnp.where(lane == 0, high, jnp.where(lane == 1, sums - high, 0.0))
    msg_ref[:, JOINT:] = parts.astype(BF16)
    return sums


def put_projection(x, own, msg_ref, own_ref, sums_ref):
    own_ref[...] = own
    msg_ref[:, :JOINT] = own.astype(BF16)
    sums_ref[...] = put_sums(x, msg_ref)


def prepare_kernel(docs1_ref, docs2_ref, cos_in, sin_in, bias1_ref, bias2_ref, cos_ref, sin_ref):
    cos_ref[...] = cos_in[...]
    sin_ref[...] = sin_in[...]
    key = lax.broadcasted_iota(jnp.int32, (T, T), 0)
    query = lax.broadcasted_iota(jnp.int32, (T, T), 1)
    for docs_ref, bias_ref in ((docs1_ref, bias1_ref), (docs2_ref, bias2_ref)):
        of_query = jnp.broadcast_to(docs_ref[...], (T, T))
        same = jnp.transpose(of_query) == of_query
        bias_ref[...] = jnp.where((key <= query) & same, 0.0, -1e30)


def group_pair(block, half):
    low = lane_index(block.shape) < 64
    if half == 0:
        first = jnp.where(low, block, 0.0)
        return jnp.concatenate([first, pltpu.roll(first, 64, 1)], axis=0)
    second = jnp.where(low, 0.0, block)
    return jnp.concatenate([pltpu.roll(second, 64, 1), second], axis=0)


def group_pair_back(turned, half):
    part = turned[64 * half : 64 * half + 64]
    zero = jnp.zeros_like(part)
    return jnp.concatenate(
        [jnp.concatenate([part, zero], axis=1), jnp.concatenate([zero, part], axis=1)], axis=0
    )


def stack_pairs(blocks, group):
    return jnp.concatenate([blocks[2 * group], blocks[2 * group + 1]], axis=0)


def attend_kernel(
    stream, turn, msg_ref, own_ref, sums_ref, x_ref, w_ref, w_t_ref, bias_ref, *rest
):
    cos_ref, sin_ref = rest[:2]
    before = rest[2 : 2 + 2 * stream]
    outs = rest[2 + 2 * stream :]
    out_ref, att_ref, q_ref, k_ref, v_ref, p_ref, scale_ref = outs[:7]
    seen = R * (stream + 1)
    rows = slice(seen - R, seen)
    received = jnp.sum(msg_ref[:, JOINT:].astype(F32), axis=1, keepdims=True)
    scale = lax.rsqrt((sums_ref[...] + received) / MODEL_WIDTH + EPS)
    scale_ref[...] = scale
    cosine, sine = cos_ref[rows], sin_ref[rows]

    def column(index):
        cols = columns(index)
        return (own_ref[:, cols] + msg_ref[:, cols].astype(F32)) * scale

    ks = [rotate(column(8 + i), cosine, sine) for i in range(2)]
    vs = [column(10 + i) for i in range(2)]
    for i in range(2):
        k_ref[:, columns(i)] = ks[i].astype(BF16)
        v_ref[:, columns(i)] = vs[i].astype(BF16)
        if stream:
            ks[i] = jnp.concatenate([before[0][:, columns(i)].astype(F32), ks[i]], axis=0)
            vs[i] = jnp.concatenate([before[1][:, columns(i)].astype(F32), vs[i]], axis=0)
    qs = []
    for i in range(8):
        q = (rotate(column(i), cosine, sine) * (0.125 * LOG2E)).astype(BF16)
        q_ref[:, columns(i)] = q
        qs.append(q)
    bias = wide(bias_ref[:seen, rows], T)
    scores = [
        dot(group_pair(ks[g // 2], g % 2).astype(BF16), stack_pairs(qs, g), NT) for g in range(4)
    ]
    turned = [jnp.transpose(v).astype(BF16) for v in vs]
    for g in range(4):
        ps = []
        for half in range(2):
            part = scores[g][seen * half : seen * half + seen] + bias
            weights = jnp.exp2(part - jnp.max(part, axis=0, keepdims=True))
            weights = weights * (1.0 / jnp.sum(weights, axis=0, keepdims=True))
            ps.append(weights.astype(BF16))
            start = (2 * g + half) * seen
            p_ref[start : start + seen, :] = ps[-1]
        out = dot(group_pair_back(turned[g // 2], g % 2), jnp.concatenate(ps, axis=0))
        out = jnp.transpose(out).astype(BF16)
        att_ref[:, columns(2 * g)] = out[:R]
        att_ref[:, columns(2 * g + 1)] = out[R:]
    x = x_ref[rows] if x_ref.shape[0] == T else x_ref[...]
    out = (x.astype(F32) + dot(att_ref[...], w_ref[...])).astype(BF16)
    out_ref[...] = out
    if turn:
        own = dot(out, w_t_ref[...])
        outs[7][...] = own.astype(BF16)
        outs[8][...] = own


def attend_back(stream, with_sums, recv_ref, own_ref, q_ref, p_ref, cos_ref, sin_ref, kv, partial_refs, pg_ref):
    seen = R * (stream + 1)
    cosine, sine = cos_ref[seen - R : seen], sin_ref[seen - R : seen]
    ks, vs = [], []
    for i in range(2):
        cols = columns(i)
        ks.append(jnp.concatenate([r[:, cols] for r in kv[0::2]], axis=0).astype(F32))
        vs.append(jnp.concatenate([r[:, cols] for r in kv[1::2]], axis=0).astype(F32))
    grads = [own_ref[:, columns(i)] + recv_ref[:, columns(i)].astype(F32) for i in range(8)]
    low = lane_index((T, 128)) < 64
    dps = [
        dot(group_pair(vs[g // 2], g % 2).astype(BF16), stack_pairs(grads, g).astype(BF16), NT)
        for g in range(4)
    ]
    turned = [jnp.transpose(k).astype(BF16) for k in ks]
    total = jnp.zeros((R, 128), F32)
    dks, dvs = [], []
    for g in range(4):
        dss, ps = [], []
        for half in range(2):
            start = (2 * g + half) * seen
            weights = p_ref[start : start + seen, :]
            wide_weights = weights.astype(F32)
            product = wide_weights * dps[g][seen * half : seen * half + seen]
            ds = product - wide_weights * jnp.sum(product, axis=0, keepdims=True)
            dss.append(ds.astype(BF16))
            ps.append(weights)
        q = jnp.concatenate([q_ref[:, columns(2 * g)], q_ref[:, columns(2 * g + 1)]], axis=0)
        q = q.astype(F32)
        grad = stack_pairs(grads, g)
        sides = []
        for value in (q, grad):
            first = jnp.where(low, value, 0.0).astype(BF16)
            second = jnp.where(low, 0.0, value).astype(BF16)
            sides.append(jnp.concatenate([first, second], axis=0))
        dk = dot(jnp.concatenate(dss, axis=1), sides[0])
        dv = dot(jnp.concatenate(ps, axis=1), sides[1])
        dks.append(dk + pltpu.roll(dk, 64, 1))
        dvs.append(dv + pltpu.roll(dv, 64, 1))
        dq = jnp.transpose(dot(group_pair_back(turned[g // 2], g % 2), jnp.concatenate(dss, axis=0)))
        if with_sums:
            product = dq * q
            total = total + product[:R] + product[R:]
        for i in range(2):
            block = dq[R * i : R * i + R] * 0.125
            pg_ref[:, columns(2 * g + i)] = rotate_back(block, cosine, sine).astype(BF16)
    total = total * (1.0 / LOG2E)
    low = lane_index((seen, 128)) < 64
    for i in range(2):
        dk = jnp.where(low, dks[2 * i], dks[2 * i + 1]) * (1.0 / LOG2E)
        dv = jnp.where(low, dvs[2 * i], dvs[2 * i + 1])
        cols = columns(i)
        if stream:
            partial_refs[0][:, cols], partial_refs[1][:, cols] = dk[:R], dv[:R]
            dk, dv = dk[R:], dv[R:]
        else:
            dk, dv = dk + partial_refs[0][:, cols], dv + partial_refs[1][:, cols]
        if with_sums:
            total = total + dk * ks[i][-R:] + dv * vs[i][-R:]
        pg_ref[:, columns(8 + i)] = rotate_back(dk, cosine, sine).astype(BF16)
        pg_ref[:, columns(10 + i)] = dv.astype(BF16)
    return total


def attend_back_kernel(stream, with_input, *refs):
    count = 2 * (stream + 1)
    fixed, kv, rest = refs[:6], refs[6 : 6 + count], list(refs[6 + count :])
    if not stream:
        partials, rest = rest[:2], rest[2:]
    if with_input:
        (w_t_ref, x_ref, gain_ref, scale_ref, up_ref), rest = rest[:5], rest[5:]
    pg_ref, rest = rest[0], rest[1:]
    if stream:
        partials, rest = rest[:2], rest[2:]
    total = attend_back(stream, with_input, *fixed, kv, partials, pg_ref)
    if with_input:
        (out_ref,) = rest
        sums = jnp.sum(total, axis=1, keepdims=True) / MODEL_WIDTH
        grad = dot(pg_ref[...], w_t_ref[...])
        scale = scale_ref[...]
        out = up_ref[...].astype(F32) + wide(scale, HALF) * (gain_ref[...].astype(F32) * grad)
        factor = wide(scale * scale * sums, HALF)
        out_ref[...] = (out - x_ref[...].astype(F32) * factor).astype(BF16)


def output_back_kernel(up_ref, w_t_ref, msg_ref, own_ref):
    own = dot(up_ref[...], w_t_ref[...])
    msg_ref[...] = own.astype(BF16)
    own_ref[...] = own


def output_weight_kernel(*refs):
    att = jnp.concatenate([r[...] for r in refs[:4]], axis=0)
    up = jnp.concatenate([r[...] for r in refs[4:8]], axis=0)
    refs[8][...] = dot(att, up, TN).astype(BF16)


def gained(x, scale_ref, gain_ref):
    return (x.astype(F32) * wide(scale_ref[...], HALF) * gain_ref[...].astype(F32)).astype(BF16)


def early_weight_kernel(
    x1_ref, x2a_ref, x2b_ref, s1a_ref, s1b_ref, s2a_ref, s2b_ref, gain_ref, pa_ref, pb_ref,
    acc_ref, turned_ref,
):
    second = [gained(x2a_ref[...], s2a_ref, gain_ref), gained(x2b_ref[...], s2b_ref, gain_ref)]
    pgs = jnp.concatenate([pa_ref[...], pb_ref[...]], axis=0)
    acc_ref[...] = dot(jnp.concatenate(second, axis=0), pgs, TN)
    for i, scale_ref in enumerate((s1a_ref, s1b_ref)):
        first = gained(x1_ref[R * i : R * i + R], scale_ref, gain_ref)
        turned_ref[:, columns(i)] = jnp.transpose(first)


def last_weight_kernel(acc_ref, turned_ref, pa_ref, pb_ref, out_ref, held, sems):
    pgs = jnp.concatenate([pa_ref[...], pb_ref[...]], axis=0)
    pieces = sems.shape[0]
    size = HALF // pieces
    copies = []
    for i in range(pieces):
        rows = slice(i * size, i * size + size)
        held[rows] = (acc_ref[rows] + dot(turned_ref[rows], pgs)).astype(BF16)
        place = pl.ds(i * size, size)
        copies.append(pltpu.make_async_copy(held.at[place], out_ref.at[place], sems.at[i]))
        copies[-1].start()
    for copy in copies:
        copy.wait()


MIB = 1024 * 1024
PARAMS = pltpu.CompilerParams(vmem_limit_bytes=20 * MIB)
FIRST = pltpu.CompilerParams(vmem_limit_bytes=62 * MIB + MIB // 8)


def shape_of(dtype, *shape):
    return jax.ShapeDtypeStruct(shape, dtype)


def block(*shape):
    return pl.BlockSpec(shape, lambda i: (0,) * len(shape))


def call(kernel, args, outs, name, specs=None, out_specs=None, scratch=(), params=PARAMS, flops=1):
    specs = specs or {}
    return pl.pallas_call(
        kernel,
        grid=(1,),
        in_specs=[specs.get(i) or block(*a.shape) for i, a in enumerate(args)],
        out_specs=out_specs or [block(*o.shape) for o in outs],
        out_shape=list(outs),
        scratch_shapes=list(scratch),
        compiler_params=params,
        cost_estimate=pl.CostEstimate(flops=flops, bytes_accessed=1, transcendentals=0),
        name=name,
    )(*args)


def swap(value):
    return lax.ppermute(value, "stretch", [(0, 1), (1, 0)])


def hop(value, step):
    count = lax.axis_size("blk")
    return lax.ppermute(value, "blk", [(i, (i + step) % count) for i in range(count)])


def after(value, *others):
    return lax.optimization_barrier((value, *others))[0]


PARTS = [shape_of(BF16, R, JOINT + 128), shape_of(F32, R, JOINT), shape_of(F32, R, 128)]
IN_HBM = pl.BlockSpec(memory_space=pltpu.HBM)


def project_first(x, w_in, gain):
    return call(
        project_first_kernel, [x, gain, w_in], PARTS[:1] * 2, "project_first", params=FIRST,
        specs={0: IN_HBM, 2: IN_HBM},
        scratch=[
            pltpu.VMEM((T, HALF), BF16), pltpu.VMEM((HALF, JOINT), BF16),
            pltpu.VMEM((T, JOINT), F32), pltpu.SemaphoreType.DMA, pltpu.SemaphoreType.DMA((2,)),
        ],
    )


def project(x, layer):
    w_in, _, gain = layer[:3]
    return call(project_kernel, [x, gain, w_in], PARTS, "project")


def attend(stream, turn, x, parts, layer, bias, trig, before):
    recv, own, sums = parts
    seen = R * (stream + 1)
    shapes = [
        shape_of(BF16, R, HALF), shape_of(BF16, R, HEADS), shape_of(BF16, R, HEADS),
        shape_of(BF16, R, KEYS), shape_of(BF16, R, KEYS), shape_of(BF16, 8 * seen, T),
        shape_of(F32, R, 128),
    ]
    if turn:
        shapes += [shape_of(BF16, R, HEADS), shape_of(F32, R, HEADS)]
    outs = call(
        partial(attend_kernel, stream, turn),
        [recv, own, sums, x, layer[1], layer[4], bias, *trig, *before], shapes, "attend",
        flops=10**10 if turn and not stream else 1,
    )
    out, att, q, k, v, p, scale = outs[:7]
    kept = dict(x=x, att=att, q=q, kv=[k, v], p=p, scale=scale, out=out)
    if turn:
        kept["msg"], kept["own"] = outs[7:]
    return kept


def back(stream, recv, own, kept, trig, kv, partials, layer=None):
    args = [recv, own, kept["q"], kept["p"], *trig, *kv]
    if not stream:
        args += partials
    shapes = [shape_of(BF16, R, JOINT)]
    if stream:
        shapes += [shape_of(F32, R, KEYS)] * 2
    if layer:
        args += [layer[3], kept["x"], layer[2], kept["scale"], kept["out"]]
        shapes.append(shape_of(BF16, R, HALF))
    return call(
        partial(attend_back_kernel, stream, layer is not None), args, shapes, "attend_back"
    )


def output_back(up, layer):
    return call(
        output_back_kernel, [up, layer[4]], [shape_of(BF16, R, HEADS), shape_of(F32, R, HEADS)],
        "output_back",
    )


def shards(activations, document_ids, joint_input_weights, output_weights, norm_gains):
    blk = lax.axis_index("blk")
    w_in, w_out, gain = joint_input_weights[0], output_weights[0], norm_gains
    tables_in = [jnp.asarray(t) for t in tables()]

    x1 = activations
    msg_a, msg_b = project_first(x1, w_in, gain)
    recv_a = swap(msg_a)
    recv_b = swap(msg_b)
    ids, x1, w_in, w_out, _ = lax.optimization_barrier(
        (document_ids, x1, w_in, w_out, msg_b)
    )
    next_blk = lax.rem(blk + 1, lax.axis_size("blk"))
    docs = [
        lax.dynamic_slice_in_dim(ids, i * T, T).astype(F32)[None, :] for i in (blk, next_blk)
    ]
    bias1, bias2, *trig = call(
        prepare_kernel, [*docs, *tables_in],
        [shape_of(F32, T, T)] * 2 + [shape_of(F32, T, 128)] * 2, "prepare",
    )
    x1 = after(x1, bias1)
    own_a, sums_a, own_b, sums_b, w_in_t, w_out_t = call(
        project_own_kernel, [x1, gain, w_in, w_out],
        PARTS[1:] * 2 + [shape_of(BF16, JOINT, HALF), shape_of(BF16, HALF, HEADS)], "project_own",
    )
    layer = (w_in, w_out, gain, w_in_t, w_out_t)
    a1 = attend(0, False, x1, (recv_a, own_a, sums_a), layer, bias1, trig, [])
    xa = hop(a1["out"], -1)
    msg_a, own_a, sums_a = project(xa, layer)
    recv_a = swap(msg_a)
    recv_b = after(recv_b, msg_a)
    b1 = attend(1, False, x1, (recv_b, own_b, sums_b), layer, bias1, trig, a1["kv"])
    xb = hop(b1["out"], -1)
    msg_b, own_b, sums_b = project(after(xb, msg_a), layer)
    recv_b = swap(msg_b)
    a2 = attend(0, True, xa, (recv_a, own_a, sums_a), layer, bias2, trig, [])
    recv_a = swap(a2["msg"])
    b2 = attend(1, True, xb, (recv_b, own_b, sums_b), layer, bias2, trig, a2["kv"])
    recv_b = after(swap(b2["msg"]), recv_a)
    pgb2, dka, dva, up = back(1, recv_b, b2["own"], b2, trig, a2["kv"] + b2["kv"], None, layer)
    upb = hop(up, 1)
    pga2, up = back(0, recv_a, a2["own"], a2, trig, a2["kv"], [dka, dva], layer)
    upa = hop(up, 1)

    msg_b, own_b = output_back(upb, layer)
    recv_b = swap(msg_b)
    msg_a, own_a = output_back(after(upa, msg_b), layer)
    recv_a = swap(msg_a)
    acc, turned = call(
        early_weight_kernel,
        [x1, xa, xb, a1["scale"], b1["scale"], a2["scale"], b2["scale"], gain, pga2, pgb2],
        [shape_of(F32, HALF, JOINT), shape_of(BF16, HALF, T)], "early_weights",
    )
    (total_out,) = call(
        output_weight_kernel,
        [k["att"] for k in (a1, b1, a2, b2)] + [upa, upb, a2["out"], b2["out"]],
        [shape_of(BF16, HEADS, HALF)], "output_weights",
    )
    pgb1, dka, dva = back(1, recv_b, own_b, b1, trig, a1["kv"] + b1["kv"], None)
    (pga1,) = back(0, recv_a, own_a, a1, trig, a1["kv"], [dka, dva])
    (total_in,) = call(
        last_weight_kernel, [acc, turned, pga1, pgb1], [shape_of(BF16, HALF, JOINT)],
        "last_weights", out_specs=[IN_HBM],
        scratch=[pltpu.VMEM((HALF, JOINT), BF16), pltpu.SemaphoreType.DMA((8,))],
    )
    return (total_in[None], total_out[None])


def solution(mesh):
    placed = (
        P("blk", "stretch"),
        P(),
        P("blk", "stretch", None),
        P("blk", None, "stretch"),
        P("blk", "stretch"),
    )
    return jax.shard_map(
        shards,
        mesh=mesh,
        in_specs=placed,
        out_specs=(P("blk", "stretch", None), P("blk", None, "stretch")),
        check_vma=False,
    )
```

```python
from functools import partial

import numpy as np
import jax
import jax.numpy as jnp
from jax import lax
from jax.experimental import pallas as pl
from jax.experimental.pallas import tpu as pltpu
from jax.sharding import PartitionSpec as P

MODEL_WIDTH = 2048
HEAD_WIDTH = 64
EPS = 1e-05
THETA = 10000.0
F32, BF16 = jnp.float32, jnp.bfloat16

T = 256
R = 128
HALF = 1024
HEADS = 1024
KEYS = 256
JOINT = HEADS + 2 * KEYS
PART = JOINT // 2
LOG2E = 1.4426950408889634

NN = (((1,), (0,)), ((), ()))
NT = (((1,), (1,)), ((), ()))
TN = (((0,), (0,)), ((), ()))


def dot(left, right, dims=NN):
    return lax.dot_general(left, right, dims, preferred_element_type=F32)


def tables():
    lane = np.arange(128)
    angles = np.arange(T)[:, None] * THETA ** (-2.0 * (lane % 32) / HEAD_WIDTH)[None, :]
    sign = np.where(lane % 64 < 32, -1.0, 1.0)[None, :]
    return np.cos(angles).astype(np.float32), (np.sin(angles) * sign).astype(np.float32)


def lane_index(shape):
    return lax.broadcasted_iota(jnp.int32, shape, 1)


def exchange_halves(block):
    first = lane_index(block.shape) % 64 < 32
    return jnp.where(first, pltpu.roll(block, 96, 1), pltpu.roll(block, 32, 1))


def rotate(block, cosine, sine):
    return block * cosine + exchange_halves(block) * sine


def rotate_back(block, cosine, sine):
    return block * cosine - exchange_halves(block) * sine


def wide(tile, width):
    return jnp.concatenate([tile] * (width // 128), axis=1)


def columns(index):
    return slice(128 * index, 128 * index + 128)


def project_first_kernel(x_in, gain_ref, w_in, *rest):
    outs, (x_ref, w_ref, held, x_sem, w_sems) = rest[:2], rest[2:]
    pieces = w_sems.shape[0]
    size = HALF // pieces
    copies = [pltpu.make_async_copy(x_in, x_ref, x_sem)]
    for i in range(pieces):
        rows = pl.ds(i * size, size)
        copies.append(pltpu.make_async_copy(w_in.at[rows], w_ref.at[rows], w_sems.at[i]))
    for copy in copies:
        copy.start()
    copies[0].wait()
    x = x_ref[...].astype(F32)
    normed = (x * gain_ref[...].astype(F32)).astype(BF16)
    for stream in range(2):
        put_sums(x[R * stream : R * stream + R], outs[stream])
    for i in range(pieces):
        copies[1 + i].wait()
        part = dot(normed[:, i * size : i * size + size], w_ref[i * size : i * size + size, :])
        if i:
            part = held[...] + part
        if i < pieces - 1:
            held[...] = part
    for stream in range(2):
        outs[stream][:, :JOINT] = part[R * stream : R * stream + R].astype(BF16)


def half_pieces(half):
    return ((512 * half, 512), (HEADS + 128 * half, 128), (HEADS + KEYS + 128 * half, 128))


def project_own_kernel(x_ref, gain_ref, w_ref, w_out_ref, *rest):
    outs, w_t_ref, w_out_t_ref = rest[:4], rest[4], rest[5]
    x = x_ref[...].astype(F32)
    own = dot((x * gain_ref[...].astype(F32)).astype(BF16), w_ref[...])
    for stream in range(2):
        rows = slice(R * stream, R * stream + R)
        outs[2 * stream][...] = own[rows]
        outs[2 * stream + 1][...] = token_sums(x[rows])
    place = 0
    for start, size in half_pieces(0) + half_pieces(1):
        w_t_ref[place : place + size, :] = jnp.transpose(w_ref[:, start : start + size])
        place += size
    w_out_t_ref[...] = jnp.transpose(w_out_ref[...])


def project_kernel(x_ref, gain_ref, w_ref, *outs):
    x = x_ref[...].astype(F32)
    normed = (x * gain_ref[...].astype(F32)).astype(BF16)
    put_projection(x, dot(normed, w_ref[...]), *outs)


def token_sums(x):
    return jnp.broadcast_to(jnp.sum(x * x, axis=1, keepdims=True), (R, 128))


def put_sums(x, msg_ref):
    sums = token_sums(x)
    high = sums.astype(BF16).astype(F32)
    lane = lane_index((R, 128))
    parts = jnp.where(lane == 0, high, jnp.where(lane == 1, sums - high, 0.0))
    msg_ref[:, JOINT:] = parts.astype(BF16)
    return sums


def put_projection(x, own, msg_ref, own_ref, sums_ref):
    own_ref[...] = own
    msg_ref[:, :JOINT] = own.astype(BF16)
    sums_ref[...] = put_sums(x, msg_ref)


def prepare_kernel(docs1_ref, docs2_ref, cos_in, sin_in, bias1_ref, bias2_ref, cos_ref, sin_ref):
    cos_ref[...] = cos_in[...]
    sin_ref[...] = sin_in[...]
    key = lax.broadcasted_iota(jnp.int32, (T, T), 0)
    query = lax.broadcasted_iota(jnp.int32, (T, T), 1)
    for docs_ref, bias_ref in ((docs1_ref, bias1_ref), (docs2_ref, bias2_ref)):
        of_query = jnp.broadcast_to(docs_ref[...], (T, T))
        same = jnp.transpose(of_query) == of_query
        bias_ref[...] = jnp.where((key <= query) & same, 0.0, -1e30)


def group_pair(block, half):
    low = lane_index(block.shape) < 64
    if half == 0:
        first = jnp.where(low, block, 0.0)
        return jnp.concatenate([first, pltpu.roll(first, 64, 1)], axis=0)
    second = jnp.where(low, 0.0, block)
    return jnp.concatenate([pltpu.roll(second, 64, 1), second], axis=0)


def group_pair_back(turned, half):
    part = turned[64 * half : 64 * half + 64]
    zero = jnp.zeros_like(part)
    return jnp.concatenate(
        [jnp.concatenate([part, zero], axis=1), jnp.concatenate([zero, part], axis=1)], axis=0
    )


def stack_pairs(blocks, group):
    return jnp.concatenate([blocks[2 * group], blocks[2 * group + 1]], axis=0)


def attend_kernel(
    stream, turn, msg_ref, own_ref, sums_ref, x_ref, w_ref, w_t_ref, bias_ref, *rest
):
    cos_ref, sin_ref = rest[:2]
    before = rest[2 : 2 + 2 * stream]
    outs = rest[2 + 2 * stream :]
    out_ref, att_ref, q_ref, k_ref, v_ref, p_ref, scale_ref = outs[:7]
    seen = R * (stream + 1)
    rows = slice(seen - R, seen)
    received = jnp.sum(msg_ref[:, JOINT:].astype(F32), axis=1, keepdims=True)
    scale = lax.rsqrt((sums_ref[...] + received) / MODEL_WIDTH + EPS)
    scale_ref[...] = scale
    cosine, sine = cos_ref[rows], sin_ref[rows]

    def column(index):
        cols = columns(index)
        return (own_ref[:, cols] + msg_ref[:, cols].astype(F32)) * scale

    ks = [rotate(column(8 + i), cosine, sine) for i in range(2)]
    vs = [column(10 + i) for i in range(2)]
    for i in range(2):
        k_ref[:, columns(i)] = ks[i].astype(BF16)
        v_ref[:, columns(i)] = vs[i].astype(BF16)
        if stream:
            ks[i] = jnp.concatenate([before[0][:, columns(i)].astype(F32), ks[i]], axis=0)
            vs[i] = jnp.concatenate([before[1][:, columns(i)].astype(F32), vs[i]], axis=0)
    qs = []
    for i in range(8):
        q = (rotate(column(i), cosine, sine) * (0.125 * LOG2E)).astype(BF16)
        q_ref[:, columns(i)] = q
        qs.append(q)
    bias = wide(bias_ref[:seen, rows], T)
    scores = [
        dot(group_pair(ks[g // 2], g % 2).astype(BF16), stack_pairs(qs, g), NT) for g in range(4)
    ]
    turned = [jnp.transpose(v).astype(BF16) for v in vs]
    for g in range(4):
        ps = []
        for half in range(2):
            part = scores[g][seen * half : seen * half + seen] + bias
            weights = jnp.exp2(part - jnp.max(part, axis=0, keepdims=True))
            weights = weights * (1.0 / jnp.sum(weights, axis=0, keepdims=True))
            ps.append(weights.astype(BF16))
            start = (2 * g + half) * seen
            p_ref[start : start + seen, :] = ps[-1]
        out = dot(group_pair_back(turned[g // 2], g % 2), jnp.concatenate(ps, axis=0))
        out = jnp.transpose(out).astype(BF16)
        att_ref[:, columns(2 * g)] = out[:R]
        att_ref[:, columns(2 * g + 1)] = out[R:]
    x = x_ref[rows] if x_ref.shape[0] == T else x_ref[...]
    out = (x.astype(F32) + dot(att_ref[...], w_ref[...])).astype(BF16)
    out_ref[...] = out
    if turn:
        own = dot(out, w_t_ref[...])
        put_message(own, outs[8:])
        outs[7][...] = own


def put_message(own, msg_refs):
    width = own.shape[1] // len(msg_refs)
    for i, msg_ref in enumerate(msg_refs):
        msg_ref[...] = own[:, i * width : i * width + width].astype(BF16)


def attend_back(stream, half, r, kv, with_sums):
    seen = R * (stream + 1)
    cosine, sine = r["cos"][seen - R : seen], r["sin"][seen - R : seen]
    k, v = (
        jnp.concatenate([ref[:, columns(half)] for ref in kv[i::2]], axis=0).astype(F32)
        for i in range(2)
    )
    cols = [columns(4 * half + i) for i in range(4)]
    if "recv" in r:
        received = [r["recv"][:, c] for c in cols]
    else:
        received = [r["recv%d" % half][:, columns(i)] for i in range(4)]
    grads = [r["own"][:, c] + piece.astype(F32) for c, piece in zip(cols, received)]
    low = lane_index((T, 128)) < 64
    dps = [
        dot(group_pair(v, g).astype(BF16), stack_pairs(grads, g).astype(BF16), NT)
        for g in range(2)
    ]
    turned = jnp.transpose(k).astype(BF16)
    total = jnp.zeros((R, 128), F32)
    pg_ref, p_ref = r["pg%d" % half], r["p"]
    dks, dvs = [], []
    for g in range(2):
        dss, ps = [], []
        for side in range(2):
            start = (4 * half + 2 * g + side) * seen
            weights = p_ref[start : start + seen, :]
            wide_weights = weights.astype(F32)
            product = wide_weights * dps[g][seen * side : seen * side + seen]
            ds = product - wide_weights * jnp.sum(product, axis=0, keepdims=True)
            dss.append(ds.astype(BF16))
            ps.append(weights)
        q = jnp.concatenate([r["q"][:, cols[2 * g]], r["q"][:, cols[2 * g + 1]]], axis=0)
        q = q.astype(F32)
        grad = stack_pairs(grads, g)
        sides = []
        for value in (q, grad):
            first = jnp.where(low, value, 0.0).astype(BF16)
            second = jnp.where(low, 0.0, value).astype(BF16)
            sides.append(jnp.concatenate([first, second], axis=0))
        dk = dot(jnp.concatenate(dss, axis=1), sides[0])
        dv = dot(jnp.concatenate(ps, axis=1), sides[1])
        dks.append(dk + pltpu.roll(dk, 64, 1))
        dvs.append(dv + pltpu.roll(dv, 64, 1))
        dq = jnp.transpose(dot(group_pair_back(turned, g), jnp.concatenate(dss, axis=0)))
        if with_sums:
            product = dq * q
            total = total + product[:R] + product[R:]
        for i in range(2):
            part = dq[R * i : R * i + R] * 0.125
            pg_ref[:, columns(2 * g + i)] = rotate_back(part, cosine, sine).astype(BF16)
    low = lane_index((seen, 128)) < 64
    dk = jnp.where(low, dks[0], dks[1]) * (1.0 / LOG2E)
    dv = jnp.where(low, dvs[0], dvs[1])
    if stream:
        r["dk%d" % half][...], r["dv%d" % half][...] = dk[:R], dv[:R]
        dk, dv = dk[R:], dv[R:]
    else:
        dk, dv = dk + r["dk%d" % half][...], dv + r["dv%d" % half][...]
    pg_ref[:, columns(4)] = rotate_back(dk, cosine, sine).astype(BF16)
    pg_ref[:, columns(5)] = dv.astype(BF16)
    return total * (1.0 / LOG2E) + dk * k[-R:] + dv * v[-R:] if with_sums else None


def attend_back_kernel(stream, halves, names, *refs):
    r = dict(zip(names, refs))
    kv = [r[name] for name in ("ka", "va", "kb", "vb")[: 2 * stream + 2]]
    total = grad = 0.0
    for half in halves:
        part = attend_back(stream, half, r, kv, "w" in r)
        if "w" in r:
            total = total + part
            grad = grad + dot(r["pg%d" % half][...], r["w"][PART * half : PART * half + PART, :])
    if "total" in r and "out" not in r:
        r["total"][...], r["grad"][...] = total, grad
    if "out" in r:
        if "total" in r:
            total, grad = total + r["total"][...], grad + r["grad"][...]
        sums = jnp.sum(total, axis=1, keepdims=True) / MODEL_WIDTH
        scale = r["scale"][...]
        out = r["up"][...].astype(F32)
        out = out + wide(scale, HALF) * (r["gain"][...].astype(F32) * grad)
        factor = wide(scale * scale * sums, HALF)
        r["out"][...] = (out - r["x"][...].astype(F32) * factor).astype(BF16)


def output_back_kernel(up_ref, w_t_ref, own_ref, *msg_refs):
    own = dot(up_ref[...], w_t_ref[...])
    own_ref[...] = own
    put_message(own, msg_refs)


def output_weight_kernel(*refs):
    att = jnp.concatenate([refs[0][...], refs[1][...]], axis=0)
    up = jnp.concatenate([refs[2][...], refs[3][...]], axis=0)
    out = dot(att, up, TN)
    if len(refs) > 5:
        out = out + refs[4][...]
    refs[-1][...] = out.astype(refs[-1].dtype)


def gained(x, scale_ref, gain_ref):
    return (x.astype(F32) * wide(scale_ref[...], HALF) * gain_ref[...].astype(F32)).astype(BF16)


def early_weight_kernel(
    x1_ref, x2a_ref, x2b_ref, s1a_ref, s1b_ref, s2a_ref, s2b_ref, gain_ref, *refs
):
    pg_refs, acc_refs, turned_ref = refs[:4], refs[4:6], refs[6]
    second = [gained(x2a_ref[...], s2a_ref, gain_ref), gained(x2b_ref[...], s2b_ref, gain_ref)]
    pgs = [jnp.concatenate([r[...] for r in pair], axis=0) for pair in (pg_refs[::2], pg_refs[1::2])]
    acc = dot(jnp.concatenate(second, axis=0), jnp.concatenate(pgs, axis=1), TN)
    acc_refs[0][...], acc_refs[1][...] = acc[:, :PART], acc[:, PART:]
    for i, scale_ref in enumerate((s1a_ref, s1b_ref)):
        first = gained(x1_ref[R * i : R * i + R], scale_ref, gain_ref)
        turned_ref[:, columns(i)] = jnp.transpose(first)


def last_weight_kernel(acc0_ref, acc1_ref, turned_ref, *refs):
    pg_refs, (out_ref, held, sems) = refs[:4], refs[4:]
    pgs = [jnp.concatenate([r[...] for r in pair], axis=0) for pair in (pg_refs[:2], pg_refs[2:])]
    pieces = sems.shape[0]
    size = HALF // pieces
    copies = []
    for i in range(pieces):
        rows = pl.ds(i * size, size)
        for half, acc_ref in enumerate((acc0_ref, acc1_ref)):
            part = (acc_ref[rows] + dot(turned_ref[rows], pgs[half])).astype(BF16)
            place = 0
            for start, width in half_pieces(half):
                held[rows, start : start + width] = part[:, place : place + width]
                place += width
        copies.append(pltpu.make_async_copy(held.at[rows], out_ref.at[rows], sems.at[i]))
        copies[-1].start()
    for copy in copies:
        copy.wait()


MIB = 1024 * 1024
PARAMS = pltpu.CompilerParams(vmem_limit_bytes=20 * MIB)
FIRST = pltpu.CompilerParams(vmem_limit_bytes=62 * MIB + MIB // 8)


def shape_of(dtype, *shape):
    return jax.ShapeDtypeStruct(shape, dtype)


def block(*shape):
    return pl.BlockSpec(shape, lambda i: (0,) * len(shape))


def call(
    kernel, args, outs, name, specs=None, out_specs=None, scratch=(), params=PARAMS, flops=1
):
    specs = specs or {}
    return pl.pallas_call(
        kernel,
        grid=(1,),
        in_specs=[specs.get(i) or block(*a.shape) for i, a in enumerate(args)],
        out_specs=out_specs or [block(*o.shape) for o in outs],
        out_shape=list(outs),
        scratch_shapes=list(scratch),
        compiler_params=params,
        cost_estimate=pl.CostEstimate(flops=flops, bytes_accessed=1, transcendentals=0),
        name=name,
    )(*args)


def swap(value):
    return lax.ppermute(value, "stretch", [(0, 1), (1, 0)])


def hop(value, step):
    count = lax.axis_size("blk")
    return lax.ppermute(value, "blk", [(i, (i + step) % count) for i in range(count)])


def after(value, *others):
    return lax.optimization_barrier((value, *others))[0]


PARTS = [shape_of(BF16, R, JOINT + 128), shape_of(F32, R, JOINT), shape_of(F32, R, 128)]
IN_HBM = pl.BlockSpec(memory_space=pltpu.HBM)


def project_first(x, w_in, gain):
    return call(
        project_first_kernel, [x, gain, w_in], PARTS[:1] * 2, "project_first", params=FIRST,
        specs={0: IN_HBM, 2: IN_HBM},
        scratch=[
            pltpu.VMEM((T, HALF), BF16), pltpu.VMEM((HALF, JOINT), BF16),
            pltpu.VMEM((T, JOINT), F32), pltpu.SemaphoreType.DMA, pltpu.SemaphoreType.DMA((2,)),
        ],
    )


def project(x, layer):
    w_in, _, gain = layer[:3]
    return call(project_kernel, [x, gain, w_in], PARTS, "project")


def attend(stream, turn, x, parts, layer, bias, trig, before, cut=1):
    recv, own, sums = parts
    seen = R * (stream + 1)
    shapes = [
        shape_of(BF16, R, HALF), shape_of(BF16, R, HEADS), shape_of(BF16, R, HEADS),
        shape_of(BF16, R, KEYS), shape_of(BF16, R, KEYS), shape_of(BF16, 8 * seen, T),
        shape_of(F32, R, 128),
    ]
    if turn:
        shapes += [shape_of(F32, R, HEADS)] + [shape_of(BF16, R, HEADS // cut)] * cut
    outs = call(
        partial(attend_kernel, stream, turn),
        [recv, own, sums, x, layer[1], layer[4], bias, *trig, *before], shapes, "attend",
        flops=10**10 if turn and not stream else 1,
    )
    out, att, q, k, v, p, scale = outs[:7]
    kept = dict(x=x, att=att, q=q, kv=[k, v], p=p, scale=scale, out=out)
    if turn:
        kept["own"], kept["msgs"] = outs[7], outs[8:]
    return kept


def back(stream, halves, recvs, own, kept, trig, kv, given=None, layer=None, begun=None):
    taken = dict(recvs, own=own, q=kept["q"], p=kept["p"], cos=trig[0], sin=trig[1])
    taken.update(zip(("ka", "va", "kb", "vb"), kv))
    taken.update(given or {})
    outs = {"pg%d" % half: shape_of(BF16, R, PART) for half in halves}
    if stream:
        outs.update({n + str(h): shape_of(F32, R, KEYS // 2) for n in ("dk", "dv") for h in halves})
    if layer:
        taken["w"] = layer[3]
        if 1 in halves:
            taken.update(x=kept["x"], gain=layer[2], scale=kept["scale"], up=kept["out"])
            taken.update(begun or {})
            outs["out"] = shape_of(BF16, R, HALF)
        else:
            outs.update(total=shape_of(F32, R, 128), grad=shape_of(F32, R, HALF))
    names = [*taken, *outs]
    done = call(
        partial(attend_back_kernel, stream, halves, names), list(taken.values()),
        list(outs.values()), "attend_back",
    )
    return dict(zip(outs, done))


def output_back(up, layer, cut=1):
    return call(
        output_back_kernel, [up, layer[4]],
        [shape_of(F32, R, HEADS)] + [shape_of(BF16, R, HEADS // cut)] * cut, "output_back",
    )


def only(outs, *names):
    return {name: value for name, value in outs.items() if name.startswith(names)}


def shards(activations, document_ids, joint_input_weights, output_weights, norm_gains):
    blk = lax.axis_index("blk")
    w_in, w_out, gain = joint_input_weights[0], output_weights[0], norm_gains
    tables_in = [jnp.asarray(t) for t in tables()]

    x1 = activations
    msg_a, msg_b = project_first(x1, w_in, gain)
    recv_a = swap(msg_a)
    recv_b = swap(msg_b)
    ids, x1, w_in, w_out, _ = lax.optimization_barrier(
        (document_ids, x1, w_in, w_out, msg_b)
    )
    next_blk = lax.rem(blk + 1, lax.axis_size("blk"))
    docs = [
        lax.dynamic_slice_in_dim(ids, i * T, T).astype(F32)[None, :] for i in (blk, next_blk)
    ]
    bias1, bias2, *trig = call(
        prepare_kernel, [*docs, *tables_in],
        [shape_of(F32, T, T)] * 2 + [shape_of(F32, T, 128)] * 2, "prepare",
    )
    x1 = after(x1, bias1)
    own_a, sums_a, own_b, sums_b, w_in_t, w_out_t = call(
        project_own_kernel, [x1, gain, w_in, w_out],
        PARTS[1:] * 2 + [shape_of(BF16, JOINT, HALF), shape_of(BF16, HALF, HEADS)], "project_own",
    )
    layer = (w_in, w_out, gain, w_in_t, w_out_t)
    a1 = attend(0, False, x1, (recv_a, own_a, sums_a), layer, bias1, trig, [])
    xa = hop(a1["out"], -1)
    msg_a, own_a, sums_a = project(xa, layer)
    recv_a = swap(msg_a)
    recv_b = after(recv_b, msg_a)
    b1 = attend(1, False, x1, (recv_b, own_b, sums_b), layer, bias1, trig, a1["kv"])
    xb = hop(b1["out"], -1)
    msg_b, own_b, sums_b = project(after(xb, msg_a), layer)
    recv_b = swap(msg_b)
    a2 = attend(0, True, xa, (recv_a, own_a, sums_a), layer, bias2, trig, [])
    recv_a = swap(a2["msgs"][0])
    b2 = attend(
        1, True, xb, (recv_b, own_b, sums_b), layer, bias2, trig, a2["kv"], cut=2
    )
    begun_out = call(
        output_weight_kernel, [a2["att"], b2["att"], a2["out"], b2["out"]],
        [shape_of(F32, HEADS, HALF)], "output_weights",
    )[0]
    recvs_b = [swap(msg) for msg in b2["msgs"]]
    recvs_b[0] = after(recvs_b[0], recv_a, begun_out)
    kv = a2["kv"] + b2["kv"]
    first = back(1, (0,), {"recv0": recvs_b[0]}, b2["own"], b2, trig, kv, layer=layer)
    pgb2 = back(
        1, (1,), {"recv1": recvs_b[1]}, b2["own"], b2, trig, kv, layer=layer,
        begun=only(first, "total", "grad"),
    )
    pgb2.update(only(first, "pg", "d"))
    upb = hop(pgb2["out"], 1)
    pga2 = back(
        0, (0, 1), {"recv": recv_a}, a2["own"], a2, trig, a2["kv"], only(pgb2, "d"), layer
    )
    upa = hop(pga2["out"], 1)

    *accs, turned = call(
        early_weight_kernel,
        [
            x1, xa, xb, a1["scale"], b1["scale"], a2["scale"], b2["scale"], gain,
            pga2["pg0"], pga2["pg1"], pgb2["pg0"], pgb2["pg1"],
        ],
        [shape_of(F32, HALF, PART)] * 2 + [shape_of(BF16, HALF, T)], "early_weights",
    )
    own_b, msg_b = output_back(after(upb, turned), layer)
    recv_b = swap(msg_b)
    own_a, *msgs_a = output_back(after(upa, msg_b), layer, 2)
    recvs_a = [swap(msg) for msg in msgs_a]
    (total_out,) = call(
        output_weight_kernel, [a1["att"], b1["att"], upa, upb, begun_out],
        [shape_of(BF16, HEADS, HALF)], "output_weights",
    )
    pgb1 = back(1, (0, 1), {"recv": recv_b}, own_b, b1, trig, a1["kv"] + b1["kv"])
    pga1 = {}
    for half in range(2):
        pga1.update(
            back(
                0, (half,), {"recv%d" % half: recvs_a[half]}, own_a, a1, trig, a1["kv"],
                only(pgb1, "dk%d" % half, "dv%d" % half),
            )
        )
    (total_in,) = call(
        last_weight_kernel,
        [*accs, turned, pga1["pg0"], pgb1["pg0"], pga1["pg1"], pgb1["pg1"]],
        [shape_of(BF16, HALF, JOINT)], "last_weights", out_specs=[IN_HBM],
        scratch=[pltpu.VMEM((HALF, JOINT), BF16), pltpu.SemaphoreType.DMA((8,))],
    )
    return (total_in[None], total_out[None])


def solution(mesh):
    placed = (
        P("blk", "stretch"),
        P(),
        P("blk", "stretch", None),
        P("blk", None, "stretch"),
        P("blk", "stretch"),
    )
    return jax.shard_map(
        shards,
        mesh=mesh,
        in_specs=placed,
        out_specs=(P("blk", "stretch", None), P("blk", None, "stretch")),
        check_vma=False,
    )
```

```python
from functools import partial

import numpy as np
import jax
import jax.numpy as jnp
from jax import lax
from jax.experimental import pallas as pl
from jax.experimental.pallas import tpu as pltpu
from jax.sharding import PartitionSpec as P

MODEL_WIDTH = 2048
HEAD_WIDTH = 64
EPS = 1e-05
THETA = 10000.0
F32, BF16 = jnp.float32, jnp.bfloat16

T = 256
R = 128
HALF = 1024
HEADS = 1024
KEYS = 256
JOINT = HEADS + 2 * KEYS
PART = JOINT // 2
LOG2E = 1.4426950408889634

NN = (((1,), (0,)), ((), ()))
NT = (((1,), (1,)), ((), ()))
TN = (((0,), (0,)), ((), ()))


def dot(left, right, dims=NN):
    return lax.dot_general(left, right, dims, preferred_element_type=F32)


def tables():
    lane = np.arange(128)
    angles = np.arange(T)[:, None] * THETA ** (-2.0 * (lane % 32) / HEAD_WIDTH)[None, :]
    sign = np.where(lane % 64 < 32, -1.0, 1.0)[None, :]
    return np.cos(angles).astype(np.float32), (np.sin(angles) * sign).astype(np.float32)


def lane_index(shape):
    return lax.broadcasted_iota(jnp.int32, shape, 1)


def exchange_halves(block):
    first = lane_index(block.shape) % 64 < 32
    return jnp.where(first, pltpu.roll(block, 96, 1), pltpu.roll(block, 32, 1))


def rotate(block, cosine, sine):
    return block * cosine + exchange_halves(block) * sine


def rotate_back(block, cosine, sine):
    return block * cosine - exchange_halves(block) * sine


def wide(tile, width):
    return jnp.concatenate([tile] * (width // 128), axis=1)


def columns(index):
    return slice(128 * index, 128 * index + 128)


def project_first_kernel(x_in, gain_ref, w_in, *rest):
    outs, (x_ref, w_ref, held, x_sem, w_sems, out_sems) = rest[:2], rest[2:]
    pieces = w_sems.shape[0]
    size = JOINT // pieces
    copies = [pltpu.make_async_copy(x_in, x_ref, x_sem)]
    for i in range(pieces):
        cols = pl.ds(i * size, size)
        copies.append(pltpu.make_async_copy(w_in.at[:, cols], w_ref.at[:, cols], w_sems.at[i]))
    for copy in copies:
        copy.start()
    sent = []

    def send(piece, cols):
        for stream in range(2):
            rows = pl.ds(R * stream, R)
            sent.append(
                pltpu.make_async_copy(
                    held.at[rows, cols], outs[stream].at[:, cols], out_sems.at[stream, piece]
                )
            )
            sent[-1].start()

    copies[0].wait()
    x = x_ref[...].astype(F32)
    normed = (x * gain_ref[...].astype(F32)).astype(BF16)
    for stream in range(2):
        rows = slice(R * stream, R * stream + R)
        put_sums(x[rows], held.at[rows])
    send(pieces, pl.ds(JOINT, 128))
    for i in range(pieces):
        copies[1 + i].wait()
        cols = slice(i * size, i * size + size)
        held[:, cols] = dot(normed, w_ref[:, cols]).astype(BF16)
        send(i, pl.ds(i * size, size))
    for copy in sent:
        copy.wait()


def half_pieces(half):
    return ((512 * half, 512), (HEADS + 128 * half, 128), (HEADS + KEYS + 128 * half, 128))


def project_own_kernel(x_ref, gain_ref, w_ref, w_out_ref, *rest):
    outs, w_t_ref, w_out_t_ref = rest[:4], rest[4], rest[5]
    x = x_ref[...].astype(F32)
    own = dot((x * gain_ref[...].astype(F32)).astype(BF16), w_ref[...])
    for stream in range(2):
        rows = slice(R * stream, R * stream + R)
        outs[2 * stream][...] = own[rows]
        outs[2 * stream + 1][...] = token_sums(x[rows])
    place = 0
    for start, size in half_pieces(0) + half_pieces(1):
        w_t_ref[place : place + size, :] = jnp.transpose(w_ref[:, start : start + size])
        place += size
    w_out_t_ref[...] = jnp.transpose(w_out_ref[...])


def project_kernel(x_ref, gain_ref, w_ref, *outs):
    x = x_ref[...].astype(F32)
    normed = (x * gain_ref[...].astype(F32)).astype(BF16)
    put_projection(x, dot(normed, w_ref[...]), *outs)


def token_sums(x):
    return jnp.broadcast_to(jnp.sum(x * x, axis=1, keepdims=True), (R, 128))


def put_sums(x, msg_ref):
    sums = token_sums(x)
    high = sums.astype(BF16).astype(F32)
    lane = lane_index((R, 128))
    parts = jnp.where(lane == 0, high, jnp.where(lane == 1, sums - high, 0.0))
    msg_ref[:, JOINT:] = parts.astype(BF16)
    return sums


def put_projection(x, own, msg_ref, own_ref, sums_ref):
    own_ref[...] = own
    msg_ref[:, :JOINT] = own.astype(BF16)
    sums_ref[...] = put_sums(x, msg_ref)


def prepare_kernel(docs1_ref, docs2_ref, cos_in, sin_in, bias1_ref, bias2_ref, cos_ref, sin_ref):
    cos_ref[...] = cos_in[...]
    sin_ref[...] = sin_in[...]
    key = lax.broadcasted_iota(jnp.int32, (T, T), 0)
    query = lax.broadcasted_iota(jnp.int32, (T, T), 1)
    for docs_ref, bias_ref in ((docs1_ref, bias1_ref), (docs2_ref, bias2_ref)):
        of_query = jnp.broadcast_to(docs_ref[...], (T, T))
        same = jnp.transpose(of_query) == of_query
        bias_ref[...] = jnp.where((key <= query) & same, 0.0, -1e30)


def group_pair(block, half):
    low = lane_index(block.shape) < 64
    if half == 0:
        first = jnp.where(low, block, 0.0)
        return jnp.concatenate([first, pltpu.roll(first, 64, 1)], axis=0)
    second = jnp.where(low, 0.0, block)
    return jnp.concatenate([pltpu.roll(second, 64, 1), second], axis=0)


def group_pair_back(turned, half):
    part = turned[64 * half : 64 * half + 64]
    zero = jnp.zeros_like(part)
    return jnp.concatenate(
        [jnp.concatenate([part, zero], axis=1), jnp.concatenate([zero, part], axis=1)], axis=0
    )


def stack_pairs(blocks, group):
    return jnp.concatenate([blocks[2 * group], blocks[2 * group + 1]], axis=0)


def attend_kernel(
    stream, turn, msg_ref, own_ref, sums_ref, x_ref, w_ref, w_t_ref, bias_ref, *rest
):
    cos_ref, sin_ref = rest[:2]
    before = rest[2 : 2 + 2 * stream]
    outs = rest[2 + 2 * stream :]
    out_ref, att_ref, q_ref, k_ref, v_ref, p_ref, scale_ref = outs[:7]
    seen = R * (stream + 1)
    rows = slice(seen - R, seen)
    received = jnp.sum(msg_ref[:, JOINT:].astype(F32), axis=1, keepdims=True)
    scale = lax.rsqrt((sums_ref[...] + received) / MODEL_WIDTH + EPS)
    scale_ref[...] = scale
    cosine, sine = cos_ref[rows], sin_ref[rows]

    def column(index):
        cols = columns(index)
        return (own_ref[:, cols] + msg_ref[:, cols].astype(F32)) * scale

    ks = [rotate(column(8 + i), cosine, sine) for i in range(2)]
    vs = [column(10 + i) for i in range(2)]
    for i in range(2):
        k_ref[:, columns(i)] = ks[i].astype(BF16)
        v_ref[:, columns(i)] = vs[i].astype(BF16)
        if stream:
            ks[i] = jnp.concatenate([before[0][:, columns(i)].astype(F32), ks[i]], axis=0)
            vs[i] = jnp.concatenate([before[1][:, columns(i)].astype(F32), vs[i]], axis=0)
    qs = []
    for i in range(8):
        q = (rotate(column(i), cosine, sine) * (0.125 * LOG2E)).astype(BF16)
        q_ref[:, columns(i)] = q
        qs.append(q)
    bias = wide(bias_ref[:seen, rows], T)
    scores = [
        dot(group_pair(ks[g // 2], g % 2).astype(BF16), stack_pairs(qs, g), NT) for g in range(4)
    ]
    turned = [jnp.transpose(v).astype(BF16) for v in vs]
    for g in range(4):
        ps = []
        for half in range(2):
            part = scores[g][seen * half : seen * half + seen] + bias
            weights = jnp.exp2(part - jnp.max(part, axis=0, keepdims=True))
            weights = weights * (1.0 / jnp.sum(weights, axis=0, keepdims=True))
            ps.append(weights.astype(BF16))
            start = (2 * g + half) * seen
            p_ref[start : start + seen, :] = ps[-1]
        out = dot(group_pair_back(turned[g // 2], g % 2), jnp.concatenate(ps, axis=0))
        out = jnp.transpose(out).astype(BF16)
        att_ref[:, columns(2 * g)] = out[:R]
        att_ref[:, columns(2 * g + 1)] = out[R:]
    x = x_ref[rows] if x_ref.shape[0] == T else x_ref[...]
    out = (x.astype(F32) + dot(att_ref[...], w_ref[...])).astype(BF16)
    out_ref[...] = out
    if turn:
        own = dot(out, w_t_ref[...])
        put_message(own, outs[8:])
        outs[7][...] = own


def put_message(own, msg_refs):
    width = own.shape[1] // len(msg_refs)
    for i, msg_ref in enumerate(msg_refs):
        msg_ref[...] = own[:, i * width : i * width + width].astype(BF16)


def attend_back(stream, half, r, kv, with_sums):
    seen = R * (stream + 1)
    cosine, sine = r["cos"][seen - R : seen], r["sin"][seen - R : seen]
    k, v = (
        jnp.concatenate([ref[:, columns(half)] for ref in kv[i::2]], axis=0).astype(F32)
        for i in range(2)
    )
    cols = [columns(4 * half + i) for i in range(4)]
    if "recv" in r:
        received = [r["recv"][:, c] for c in cols]
    else:
        received = [r["recv%d" % half][:, columns(i)] for i in range(4)]
    grads = [r["own"][:, c] + piece.astype(F32) for c, piece in zip(cols, received)]
    low = lane_index((T, 128)) < 64
    dps = [
        dot(group_pair(v, g).astype(BF16), stack_pairs(grads, g).astype(BF16), NT)
        for g in range(2)
    ]
    turned = jnp.transpose(k).astype(BF16)
    total = jnp.zeros((R, 128), F32)
    pg_ref, p_ref = r["pg%d" % half], r["p"]
    dks, dvs = [], []
    for g in range(2):
        dss, ps = [], []
        for side in range(2):
            start = (4 * half + 2 * g + side) * seen
            weights = p_ref[start : start + seen, :]
            wide_weights = weights.astype(F32)
            product = wide_weights * dps[g][seen * side : seen * side + seen]
            ds = product - wide_weights * jnp.sum(product, axis=0, keepdims=True)
            dss.append(ds.astype(BF16))
            ps.append(weights)
        q = jnp.concatenate([r["q"][:, cols[2 * g]], r["q"][:, cols[2 * g + 1]]], axis=0)
        q = q.astype(F32)
        grad = stack_pairs(grads, g)
        sides = []
        for value in (q, grad):
            first = jnp.where(low, value, 0.0).astype(BF16)
            second = jnp.where(low, 0.0, value).astype(BF16)
            sides.append(jnp.concatenate([first, second], axis=0))
        dk = dot(jnp.concatenate(dss, axis=1), sides[0])
        dv = dot(jnp.concatenate(ps, axis=1), sides[1])
        dks.append(dk + pltpu.roll(dk, 64, 1))
        dvs.append(dv + pltpu.roll(dv, 64, 1))
        dq = jnp.transpose(dot(group_pair_back(turned, g), jnp.concatenate(dss, axis=0)))
        if with_sums:
            product = dq * q
            total = total + product[:R] + product[R:]
        for i in range(2):
            part = dq[R * i : R * i + R] * 0.125
            pg_ref[:, columns(2 * g + i)] = rotate_back(part, cosine, sine).astype(BF16)
    low = lane_index((seen, 128)) < 64
    dk = jnp.where(low, dks[0], dks[1]) * (1.0 / LOG2E)
    dv = jnp.where(low, dvs[0], dvs[1])
    if stream:
        r["dk%d" % half][...], r["dv%d" % half][...] = dk[:R], dv[:R]
        dk, dv = dk[R:], dv[R:]
    else:
        dk, dv = dk + r["dk%d" % half][...], dv + r["dv%d" % half][...]
    pg_ref[:, columns(4)] = rotate_back(dk, cosine, sine).astype(BF16)
    pg_ref[:, columns(5)] = dv.astype(BF16)
    return total * (1.0 / LOG2E) + dk * k[-R:] + dv * v[-R:] if with_sums else None


def attend_back_kernel(stream, halves, names, *refs):
    r = dict(zip(names, refs))
    kv = [r[name] for name in ("ka", "va", "kb", "vb")[: 2 * stream + 2]]
    total = grad = 0.0
    for half in halves:
        part = attend_back(stream, half, r, kv, "w" in r)
        if "w" in r:
            total = total + part
            grad = grad + dot(r["pg%d" % half][...], r["w"][PART * half : PART * half + PART, :])
    if "total" in r and "out" not in r:
        r["total"][...], r["grad"][...] = total, grad
    if "out" in r:
        if "total" in r:
            total, grad = total + r["total"][...], grad + r["grad"][...]
        sums = jnp.sum(total, axis=1, keepdims=True) / MODEL_WIDTH
        scale = r["scale"][...]
        out = r["up"][...].astype(F32)
        out = out + wide(scale, HALF) * (r["gain"][...].astype(F32) * grad)
        factor = wide(scale * scale * sums, HALF)
        r["out"][...] = (out - r["x"][...].astype(F32) * factor).astype(BF16)


def output_back_kernel(up_ref, w_t_ref, own_ref, *msg_refs):
    own = dot(up_ref[...], w_t_ref[...])
    own_ref[...] = own
    put_message(own, msg_refs)


def early_output_kernel(att_a_ref, att_b_ref, up_a_ref, up_b_ref, acc_ref):
    att = jnp.concatenate([att_a_ref[...], att_b_ref[...]], axis=0)
    acc_ref[...] = dot(att, jnp.concatenate([up_a_ref[...], up_b_ref[...]], axis=0), TN)


def output_weight_kernel(
    att_a_ref, att_b_ref, up_a_ref, up_b_ref, acc_ref, out_ref, held, sems
):
    up = jnp.concatenate([up_a_ref[...], up_b_ref[...]], axis=0)
    pieces = sems.shape[0]
    size = HEADS // pieces
    copies = []
    for i in range(pieces):
        rows = pl.ds(i * size, size)
        att = jnp.concatenate([att_a_ref[:, rows], att_b_ref[:, rows]], axis=0)
        held[rows] = (acc_ref[rows] + dot(att, up, TN)).astype(BF16)
        copies.append(pltpu.make_async_copy(held.at[rows], out_ref.at[rows], sems.at[i]))
        copies[-1].start()
    for copy in copies:
        copy.wait()


def gained(x, scale_ref, gain_ref):
    return (x.astype(F32) * wide(scale_ref[...], HALF) * gain_ref[...].astype(F32)).astype(BF16)


def early_weight_kernel(
    x1_ref, x2a_ref, x2b_ref, s1a_ref, s1b_ref, s2a_ref, s2b_ref, gain_ref, *refs
):
    pg_refs, acc_refs, turned_ref = refs[:4], refs[4:6], refs[6]
    second = [gained(x2a_ref[...], s2a_ref, gain_ref), gained(x2b_ref[...], s2b_ref, gain_ref)]
    pgs = [jnp.concatenate([r[...] for r in pair], axis=0) for pair in (pg_refs[::2], pg_refs[1::2])]
    acc = dot(jnp.concatenate(second, axis=0), jnp.concatenate(pgs, axis=1), TN)
    acc_refs[0][...], acc_refs[1][...] = acc[:, :PART], acc[:, PART:]
    for i, scale_ref in enumerate((s1a_ref, s1b_ref)):
        first = gained(x1_ref[R * i : R * i + R], scale_ref, gain_ref)
        turned_ref[:, columns(i)] = jnp.transpose(first)


def last_weight_kernel(acc0_ref, acc1_ref, turned_ref, *refs):
    pg_refs, (out_ref, held, sems) = refs[:4], refs[4:]
    pgs = [jnp.concatenate([r[...] for r in pair], axis=0) for pair in (pg_refs[:2], pg_refs[2:])]
    pieces = sems.shape[0]
    size = HALF // pieces
    copies = []
    for i in range(pieces):
        rows = pl.ds(i * size, size)
        for half, acc_ref in enumerate((acc0_ref, acc1_ref)):
            part = (acc_ref[rows] + dot(turned_ref[rows], pgs[half])).astype(BF16)
            place = 0
            for start, width in half_pieces(half):
                held[rows, start : start + width] = part[:, place : place + width]
                place += width
        copies.append(pltpu.make_async_copy(held.at[rows], out_ref.at[rows], sems.at[i]))
        copies[-1].start()
    for copy in copies:
        copy.wait()


MIB = 1024 * 1024
PARAMS = pltpu.CompilerParams(vmem_limit_bytes=20 * MIB)
FIRST = pltpu.CompilerParams(vmem_limit_bytes=62 * MIB + MIB // 8)


def shape_of(dtype, *shape):
    return jax.ShapeDtypeStruct(shape, dtype)


def block(*shape):
    return pl.BlockSpec(shape, lambda i: (0,) * len(shape))


def call(
    kernel, args, outs, name, specs=None, out_specs=None, scratch=(), params=PARAMS, flops=1
):
    specs = specs or {}
    return pl.pallas_call(
        kernel,
        grid=(1,),
        in_specs=[specs.get(i) or block(*a.shape) for i, a in enumerate(args)],
        out_specs=out_specs or [block(*o.shape) for o in outs],
        out_shape=list(outs),
        scratch_shapes=list(scratch),
        compiler_params=params,
        cost_estimate=pl.CostEstimate(flops=flops, bytes_accessed=1, transcendentals=0),
        name=name,
    )(*args)


def swap(value):
    return lax.ppermute(value, "stretch", [(0, 1), (1, 0)])


def hop(value, step):
    count = lax.axis_size("blk")
    return lax.ppermute(value, "blk", [(i, (i + step) % count) for i in range(count)])


def after(value, *others):
    return lax.optimization_barrier((value, *others))[0]


PARTS = [shape_of(BF16, R, JOINT + 128), shape_of(F32, R, JOINT), shape_of(F32, R, 128)]
IN_HBM = pl.BlockSpec(memory_space=pltpu.HBM)


def project_first(x, w_in, gain):
    return call(
        project_first_kernel, [x, gain, w_in], PARTS[:1] * 2, "project_first", params=FIRST,
        specs={0: IN_HBM, 2: IN_HBM}, out_specs=[IN_HBM] * 2,
        scratch=[
            pltpu.VMEM((T, HALF), BF16), pltpu.VMEM((HALF, JOINT), BF16),
            pltpu.VMEM((T, JOINT + 128), BF16), pltpu.SemaphoreType.DMA,
            pltpu.SemaphoreType.DMA((3,)), pltpu.SemaphoreType.DMA((2, 4)),
        ],
    )


def project(x, layer):
    w_in, _, gain = layer[:3]
    return call(project_kernel, [x, gain, w_in], PARTS, "project")


def attend(stream, turn, x, parts, layer, bias, trig, before, cut=1):
    recv, own, sums = parts
    seen = R * (stream + 1)
    shapes = [
        shape_of(BF16, R, HALF), shape_of(BF16, R, HEADS), shape_of(BF16, R, HEADS),
        shape_of(BF16, R, KEYS), shape_of(BF16, R, KEYS), shape_of(BF16, 8 * seen, T),
        shape_of(F32, R, 128),
    ]
    if turn:
        shapes += [shape_of(F32, R, HEADS)] + [shape_of(BF16, R, HEADS // cut)] * cut
    outs = call(
        partial(attend_kernel, stream, turn),
        [recv, own, sums, x, layer[1], layer[4], bias, *trig, *before], shapes, "attend",
        flops=10**10 if turn and not stream else 1,
    )
    out, att, q, k, v, p, scale = outs[:7]
    kept = dict(x=x, att=att, q=q, kv=[k, v], p=p, scale=scale, out=out)
    if turn:
        kept["own"], kept["msgs"] = outs[7], outs[8:]
    return kept


def back(stream, halves, recvs, own, kept, trig, kv, given=None, layer=None, begun=None):
    taken = dict(recvs, own=own, q=kept["q"], p=kept["p"], cos=trig[0], sin=trig[1])
    taken.update(zip(("ka", "va", "kb", "vb"), kv))
    taken.update(given or {})
    outs = {"pg%d" % half: shape_of(BF16, R, PART) for half in halves}
    if stream:
        outs.update({n + str(h): shape_of(F32, R, KEYS // 2) for n in ("dk", "dv") for h in halves})
    if layer:
        taken["w"] = layer[3]
        if 1 in halves:
            taken.update(x=kept["x"], gain=layer[2], scale=kept["scale"], up=kept["out"])
            taken.update(begun or {})
            outs["out"] = shape_of(BF16, R, HALF)
        else:
            outs.update(total=shape_of(F32, R, 128), grad=shape_of(F32, R, HALF))
    names = [*taken, *outs]
    done = call(
        partial(attend_back_kernel, stream, halves, names), list(taken.values()),
        list(outs.values()), "attend_back",
    )
    return dict(zip(outs, done))


def output_back(up, layer, cut=1):
    return call(
        output_back_kernel, [up, layer[4]],
        [shape_of(F32, R, HEADS)] + [shape_of(BF16, R, HEADS // cut)] * cut, "output_back",
    )


def only(outs, *names):
    return {name: value for name, value in outs.items() if name.startswith(names)}


def shards(activations, document_ids, joint_input_weights, output_weights, norm_gains):
    blk = lax.axis_index("blk")
    w_in, w_out, gain = joint_input_weights[0], output_weights[0], norm_gains
    tables_in = [jnp.asarray(t) for t in tables()]

    x1 = activations
    msg_a, msg_b = project_first(x1, w_in, gain)
    recv_a = swap(msg_a)
    recv_b = swap(msg_b)
    ids, x1, w_in, w_out, _ = lax.optimization_barrier(
        (document_ids, x1, w_in, w_out, msg_b)
    )
    next_blk = lax.rem(blk + 1, lax.axis_size("blk"))
    docs = [
        lax.dynamic_slice_in_dim(ids, i * T, T).astype(F32)[None, :] for i in (blk, next_blk)
    ]
    bias1, bias2, *trig = call(
        prepare_kernel, [*docs, *tables_in],
        [shape_of(F32, T, T)] * 2 + [shape_of(F32, T, 128)] * 2, "prepare",
    )
    x1 = after(x1, bias1)
    own_a, sums_a, own_b, sums_b, w_in_t, w_out_t = call(
        project_own_kernel, [x1, gain, w_in, w_out],
        PARTS[1:] * 2 + [shape_of(BF16, JOINT, HALF), shape_of(BF16, HALF, HEADS)], "project_own",
    )
    layer = (w_in, w_out, gain, w_in_t, w_out_t)
    a1 = attend(0, False, x1, (recv_a, own_a, sums_a), layer, bias1, trig, [])
    xa = hop(a1["out"], -1)
    msg_a, own_a, sums_a = project(xa, layer)
    recv_a = swap(msg_a)
    recv_b = after(recv_b, msg_a)
    b1 = attend(1, False, x1, (recv_b, own_b, sums_b), layer, bias1, trig, a1["kv"])
    xb = hop(b1["out"], -1)
    msg_b, own_b, sums_b = project(after(xb, msg_a), layer)
    recv_b = swap(msg_b)
    a2 = attend(0, True, xa, (recv_a, own_a, sums_a), layer, bias2, trig, [])
    recv_a = swap(a2["msgs"][0])
    b2 = attend(
        1, True, xb, (recv_b, own_b, sums_b), layer, bias2, trig, a2["kv"], cut=2
    )
    begun_out = call(
        early_output_kernel, [a2["att"], b2["att"], a2["out"], b2["out"]],
        [shape_of(F32, HEADS, HALF)], "early_output",
    )[0]
    recvs_b = [swap(msg) for msg in b2["msgs"]]
    recvs_b[0] = after(recvs_b[0], recv_a, begun_out)
    kv = a2["kv"] + b2["kv"]
    first = back(1, (0,), {"recv0": recvs_b[0]}, b2["own"], b2, trig, kv, layer=layer)
    pgb2 = back(
        1, (1,), {"recv1": recvs_b[1]}, b2["own"], b2, trig, kv, layer=layer,
        begun=only(first, "total", "grad"),
    )
    pgb2.update(only(first, "pg", "d"))
    upb = hop(pgb2["out"], 1)
    pga2 = back(
        0, (0, 1), {"recv": recv_a}, a2["own"], a2, trig, a2["kv"], only(pgb2, "d"), layer
    )
    upa = hop(pga2["out"], 1)

    *accs, turned = call(
        early_weight_kernel,
        [
            x1, xa, xb, a1["scale"], b1["scale"], a2["scale"], b2["scale"], gain,
            pga2["pg0"], pga2["pg1"], pgb2["pg0"], pgb2["pg1"],
        ],
        [shape_of(F32, HALF, PART)] * 2 + [shape_of(BF16, HALF, T)], "early_weights",
    )
    own_b, msg_b = output_back(after(upb, turned), layer)
    recv_b = swap(msg_b)
    own_a, *msgs_a = output_back(after(upa, msg_b), layer, 2)
    recvs_a = [swap(msg) for msg in msgs_a]
    (total_out,) = call(
        output_weight_kernel, [a1["att"], b1["att"], upa, upb, begun_out],
        [shape_of(BF16, HEADS, HALF)], "output_weights", out_specs=[IN_HBM],
        scratch=[pltpu.VMEM((HEADS, HALF), BF16), pltpu.SemaphoreType.DMA((8,))],
    )
    pgb1 = back(1, (0, 1), {"recv": recv_b}, own_b, b1, trig, a1["kv"] + b1["kv"])
    pga1 = {}
    for half in range(2):
        pga1.update(
            back(
                0, (half,), {"recv%d" % half: recvs_a[half]}, own_a, a1, trig, a1["kv"],
                only(pgb1, "dk%d" % half, "dv%d" % half),
            )
        )
    (total_in,) = call(
        last_weight_kernel,
        [*accs, turned, pga1["pg0"], pgb1["pg0"], pga1["pg1"], pgb1["pg1"]],
        [shape_of(BF16, HALF, JOINT)], "last_weights", out_specs=[IN_HBM],
        scratch=[pltpu.VMEM((HALF, JOINT), BF16), pltpu.SemaphoreType.DMA((8,))],
    )
    return (total_in[None], total_out[None])


def solution(mesh):
    placed = (
        P("blk", "stretch"),
        P(),
        P("blk", "stretch", None),
        P("blk", None, "stretch"),
        P("blk", "stretch"),
    )
    return jax.shard_map(
        shards,
        mesh=mesh,
        in_specs=placed,
        out_specs=(P("blk", "stretch", None), P("blk", None, "stretch")),
        check_vma=False,
    )
```

```python
from functools import partial

import numpy as np
import jax
import jax.numpy as jnp
from jax import lax
from jax.experimental import pallas as pl
from jax.experimental.pallas import tpu as pltpu
from jax.sharding import PartitionSpec as P

MODEL_WIDTH = 2048
HEAD_WIDTH = 64
EPS = 1e-05
THETA = 10000.0
F32, BF16 = jnp.float32, jnp.bfloat16

T = 256
R = 128
HALF = 1024
HEADS = 1024
KEYS = 256
JOINT = HEADS + 2 * KEYS
PART = JOINT // 2
LOG2E = 1.4426950408889634

NN = (((1,), (0,)), ((), ()))
NT = (((1,), (1,)), ((), ()))
TN = (((0,), (0,)), ((), ()))


def dot(left, right, dims=NN):
    return lax.dot_general(left, right, dims, preferred_element_type=F32)


def tables():
    lane = np.arange(128)
    angles = np.arange(T)[:, None] * THETA ** (-2.0 * (lane % 32) / HEAD_WIDTH)[None, :]
    sign = np.where(lane % 64 < 32, -1.0, 1.0)[None, :]
    return np.cos(angles).astype(np.float32), (np.sin(angles) * sign).astype(np.float32)


def lane_index(shape):
    return lax.broadcasted_iota(jnp.int32, shape, 1)


def exchange_halves(block):
    first = lane_index(block.shape) % 64 < 32
    return jnp.where(first, pltpu.roll(block, 96, 1), pltpu.roll(block, 32, 1))


def rotate(block, cosine, sine):
    return block * cosine + exchange_halves(block) * sine


def rotate_back(block, cosine, sine):
    return block * cosine - exchange_halves(block) * sine


def wide(tile, width):
    return jnp.concatenate([tile] * (width // 128), axis=1)


def columns(index):
    return slice(128 * index, 128 * index + 128)


def project_first_kernel(x_in, gain_ref, w_in, *rest):
    outs, (x_ref, w_ref, held, x_sem, w_sems) = rest[:2], rest[2:]
    pieces = w_sems.shape[0]
    size = HALF // pieces
    copies = [pltpu.make_async_copy(x_in, x_ref, x_sem)]
    for i in range(pieces):
        rows = pl.ds(i * size, size)
        copies.append(pltpu.make_async_copy(w_in.at[rows], w_ref.at[rows], w_sems.at[i]))
    for copy in copies:
        copy.start()
    copies[0].wait()
    x = x_ref[...].astype(F32)
    normed = (x * gain_ref[...].astype(F32)).astype(BF16)
    for stream in range(2):
        put_sums(x[R * stream : R * stream + R], outs[stream])
    for i in range(pieces):
        copies[1 + i].wait()
        part = dot(normed[:, i * size : i * size + size], w_ref[i * size : i * size + size, :])
        if i:
            part = held[...] + part
        if i < pieces - 1:
            held[...] = part
    for stream in range(2):
        outs[stream][:, :JOINT] = part[R * stream : R * stream + R].astype(BF16)


def half_pieces(half):
    return ((512 * half, 512), (HEADS + 128 * half, 128), (HEADS + KEYS + 128 * half, 128))


def project_own_kernel(x_ref, gain_ref, w_ref, w_out_ref, *rest):
    outs, w_t_ref, w_out_t_ref = rest[:4], rest[4], rest[5]
    x = x_ref[...].astype(F32)
    own = dot((x * gain_ref[...].astype(F32)).astype(BF16), w_ref[...])
    for stream in range(2):
        rows = slice(R * stream, R * stream + R)
        outs[2 * stream][...] = own[rows]
        outs[2 * stream + 1][...] = token_sums(x[rows])
    place = 0
    for start, size in half_pieces(0) + half_pieces(1):
        w_t_ref[place : place + size, :] = jnp.transpose(w_ref[:, start : start + size])
        place += size
    w_out_t_ref[...] = jnp.transpose(w_out_ref[...])


def project_kernel(x_ref, gain_ref, w_ref, *outs):
    x = x_ref[...].astype(F32)
    normed = (x * gain_ref[...].astype(F32)).astype(BF16)
    put_projection(x, dot(normed, w_ref[...]), *outs)


def token_sums(x):
    return jnp.broadcast_to(jnp.sum(x * x, axis=1, keepdims=True), (R, 128))


def put_sums(x, msg_ref):
    sums = token_sums(x)
    high = sums.astype(BF16).astype(F32)
    lane = lane_index((R, 128))
    parts = jnp.where(lane == 0, high, jnp.where(lane == 1, sums - high, 0.0))
    msg_ref[:, JOINT:] = parts.astype(BF16)
    return sums


def put_projection(x, own, msg_ref, own_ref, sums_ref):
    own_ref[...] = own
    msg_ref[:, :JOINT] = own.astype(BF16)
    sums_ref[...] = put_sums(x, msg_ref)


def prepare_kernel(docs1_ref, docs2_ref, cos_in, sin_in, bias1_ref, bias2_ref, cos_ref, sin_ref):
    cos_ref[...] = cos_in[...]
    sin_ref[...] = sin_in[...]
    key = lax.broadcasted_iota(jnp.int32, (T, T), 0)
    query = lax.broadcasted_iota(jnp.int32, (T, T), 1)
    for docs_ref, bias_ref in ((docs1_ref, bias1_ref), (docs2_ref, bias2_ref)):
        of_query = jnp.broadcast_to(docs_ref[...], (T, T))
        same = jnp.transpose(of_query) == of_query
        bias_ref[...] = jnp.where((key <= query) & same, 0.0, -1e30)


def group_pair(block, half):
    low = lane_index(block.shape) < 64
    if half == 0:
        first = jnp.where(low, block, 0.0)
        return jnp.concatenate([first, pltpu.roll(first, 64, 1)], axis=0)
    second = jnp.where(low, 0.0, block)
    return jnp.concatenate([pltpu.roll(second, 64, 1), second], axis=0)


def group_pair_back(turned, half):
    part = turned[64 * half : 64 * half + 64]
    zero = jnp.zeros_like(part)
    return jnp.concatenate(
        [jnp.concatenate([part, zero], axis=1), jnp.concatenate([zero, part], axis=1)], axis=0
    )


def stack_pairs(blocks, group):
    return jnp.concatenate([blocks[2 * group], blocks[2 * group + 1]], axis=0)


def attend_kernel(
    stream, turn, msg_ref, own_ref, sums_ref, x_ref, w_ref, w_t_ref, bias_ref, *rest
):
    cos_ref, sin_ref = rest[:2]
    before = rest[2 : 2 + 2 * stream]
    outs = rest[2 + 2 * stream :]
    out_ref, att_ref, q_ref, k_ref, v_ref, p_ref, scale_ref = outs[:7]
    seen = R * (stream + 1)
    rows = slice(seen - R, seen)
    received = jnp.sum(msg_ref[:, JOINT:].astype(F32), axis=1, keepdims=True)
    scale = lax.rsqrt((sums_ref[...] + received) / MODEL_WIDTH + EPS)
    scale_ref[...] = scale
    cosine, sine = cos_ref[rows], sin_ref[rows]

    def column(index):
        cols = columns(index)
        return (own_ref[:, cols] + msg_ref[:, cols].astype(F32)) * scale

    ks = [rotate(column(8 + i), cosine, sine) for i in range(2)]
    vs = [column(10 + i) for i in range(2)]
    for i in range(2):
        k_ref[:, columns(i)] = ks[i].astype(BF16)
        v_ref[:, columns(i)] = vs[i].astype(BF16)
        if stream:
            ks[i] = jnp.concatenate([before[0][:, columns(i)].astype(F32), ks[i]], axis=0)
            vs[i] = jnp.concatenate([before[1][:, columns(i)].astype(F32), vs[i]], axis=0)
    qs = []
    for i in range(8):
        q = (rotate(column(i), cosine, sine) * (0.125 * LOG2E)).astype(BF16)
        q_ref[:, columns(i)] = q
        qs.append(q)
    bias = wide(bias_ref[:seen, rows], T)
    scores = [
        dot(group_pair(ks[g // 2], g % 2).astype(BF16), stack_pairs(qs, g), NT) for g in range(4)
    ]
    turned = [jnp.transpose(v).astype(BF16) for v in vs]
    for g in range(4):
        ps = []
        for half in range(2):
            part = scores[g][seen * half : seen * half + seen] + bias
            weights = jnp.exp2(part - jnp.max(part, axis=0, keepdims=True))
            weights = weights * (1.0 / jnp.sum(weights, axis=0, keepdims=True))
            ps.append(weights.astype(BF16))
            start = (2 * g + half) * seen
            p_ref[start : start + seen, :] = ps[-1]
        out = dot(group_pair_back(turned[g // 2], g % 2), jnp.concatenate(ps, axis=0))
        out = jnp.transpose(out).astype(BF16)
        att_ref[:, columns(2 * g)] = out[:R]
        att_ref[:, columns(2 * g + 1)] = out[R:]
    x = x_ref[rows] if x_ref.shape[0] == T else x_ref[...]
    out = (x.astype(F32) + dot(att_ref[...], w_ref[...])).astype(BF16)
    out_ref[...] = out
    if turn:
        own = dot(out, w_t_ref[...])
        put_message(own, outs[8:])
        outs[7][...] = own


def put_message(own, msg_refs):
    width = own.shape[1] // len(msg_refs)
    for i, msg_ref in enumerate(msg_refs):
        msg_ref[...] = own[:, i * width : i * width + width].astype(BF16)


def attend_back(stream, half, r, kv, with_sums):
    seen = R * (stream + 1)
    cosine, sine = r["cos"][seen - R : seen], r["sin"][seen - R : seen]
    k, v = (
        jnp.concatenate([ref[:, columns(half)] for ref in kv[i::2]], axis=0).astype(F32)
        for i in range(2)
    )
    cols = [columns(4 * half + i) for i in range(4)]
    if "recv" in r:
        received = [r["recv"][:, c] for c in cols]
    else:
        received = [r["recv%d" % half][:, columns(i)] for i in range(4)]
    grads = [r["own"][:, c] + piece.astype(F32) for c, piece in zip(cols, received)]
    low = lane_index((T, 128)) < 64
    dps = [
        dot(group_pair(v, g).astype(BF16), stack_pairs(grads, g).astype(BF16), NT)
        for g in range(2)
    ]
    turned = jnp.transpose(k).astype(BF16)
    total = jnp.zeros((R, 128), F32)
    pg_ref, p_ref = r["pg%d" % half], r["p"]
    dks, dvs = [], []
    for g in range(2):
        dss, ps = [], []
        for side in range(2):
            start = (4 * half + 2 * g + side) * seen
            weights = p_ref[start : start + seen, :]
            wide_weights = weights.astype(F32)
            product = wide_weights * dps[g][seen * side : seen * side + seen]
            ds = product - wide_weights * jnp.sum(product, axis=0, keepdims=True)
            dss.append(ds.astype(BF16))
            ps.append(weights)
        q = jnp.concatenate([r["q"][:, cols[2 * g]], r["q"][:, cols[2 * g + 1]]], axis=0)
        q = q.astype(F32)
        grad = stack_pairs(grads, g)
        sides = []
        for value in (q, grad):
            first = jnp.where(low, value, 0.0).astype(BF16)
            second = jnp.where(low, 0.0, value).astype(BF16)
            sides.append(jnp.concatenate([first, second], axis=0))
        dk = dot(jnp.concatenate(dss, axis=1), sides[0])
        dv = dot(jnp.concatenate(ps, axis=1), sides[1])
        dks.append(dk + pltpu.roll(dk, 64, 1))
        dvs.append(dv + pltpu.roll(dv, 64, 1))
        dq = jnp.transpose(dot(group_pair_back(turned, g), jnp.concatenate(dss, axis=0)))
        if with_sums:
            product = dq * q
            total = total + product[:R] + product[R:]
        for i in range(2):
            part = dq[R * i : R * i + R] * 0.125
            pg_ref[:, columns(2 * g + i)] = rotate_back(part, cosine, sine).astype(BF16)
    low = lane_index((seen, 128)) < 64
    dk = jnp.where(low, dks[0], dks[1]) * (1.0 / LOG2E)
    dv = jnp.where(low, dvs[0], dvs[1])
    if stream:
        r["dk%d" % half][...], r["dv%d" % half][...] = dk[:R], dv[:R]
        dk, dv = dk[R:], dv[R:]
    else:
        dk, dv = dk + r["dk%d" % half][...], dv + r["dv%d" % half][...]
    pg_ref[:, columns(4)] = rotate_back(dk, cosine, sine).astype(BF16)
    pg_ref[:, columns(5)] = dv.astype(BF16)
    return total * (1.0 / LOG2E) + dk * k[-R:] + dv * v[-R:] if with_sums else None


def attend_back_kernel(stream, halves, names, *refs):
    r = dict(zip(names, refs))
    kv = [r[name] for name in ("ka", "va", "kb", "vb")[: 2 * stream + 2]]
    total = grad = 0.0
    for half in halves:
        part = attend_back(stream, half, r, kv, "w" in r)
        if "w" in r:
            total = total + part
            grad = grad + dot(r["pg%d" % half][...], r["w"][PART * half : PART * half + PART, :])
    if "total" in r and "out" not in r:
        r["total"][...], r["grad"][...] = total, grad
    if "out" in r:
        if "total" in r:
            total, grad = total + r["total"][...], grad + r["grad"][...]
        sums = jnp.sum(total, axis=1, keepdims=True) / MODEL_WIDTH
        scale = r["scale"][...]
        out = r["up"][...].astype(F32)
        out = out + wide(scale, HALF) * (r["gain"][...].astype(F32) * grad)
        factor = wide(scale * scale * sums, HALF)
        r["out"][...] = (out - r["x"][...].astype(F32) * factor).astype(BF16)


def output_back_kernel(up_ref, w_t_ref, own_ref, *msg_refs):
    own = dot(up_ref[...], w_t_ref[...])
    own_ref[...] = own
    put_message(own, msg_refs)


def early_output_kernel(att_a_ref, att_b_ref, up_a_ref, up_b_ref, acc_ref):
    att = jnp.concatenate([att_a_ref[...], att_b_ref[...]], axis=0)
    acc_ref[...] = dot(att, jnp.concatenate([up_a_ref[...], up_b_ref[...]], axis=0), TN)


def output_weight_kernel(
    att_a_ref, att_b_ref, up_a_ref, up_b_ref, acc_ref, out_ref, held, sems
):
    up = jnp.concatenate([up_a_ref[...], up_b_ref[...]], axis=0)
    pieces = sems.shape[0]
    size = HEADS // pieces
    copies = []
    for i in range(pieces):
        rows = pl.ds(i * size, size)
        att = jnp.concatenate([att_a_ref[:, rows], att_b_ref[:, rows]], axis=0)
        held[rows] = (acc_ref[rows] + dot(att, up, TN)).astype(BF16)
        copies.append(pltpu.make_async_copy(held.at[rows], out_ref.at[rows], sems.at[i]))
        copies[-1].start()
    for copy in copies:
        copy.wait()


def gained(x, scale_ref, gain_ref):
    return (x.astype(F32) * wide(scale_ref[...], HALF) * gain_ref[...].astype(F32)).astype(BF16)


def early_weight_kernel(
    x1_ref, x2a_ref, x2b_ref, s1a_ref, s1b_ref, s2a_ref, s2b_ref, gain_ref, *refs
):
    pg_refs, acc_refs, turned_ref = refs[:4], refs[4:6], refs[6]
    second = [gained(x2a_ref[...], s2a_ref, gain_ref), gained(x2b_ref[...], s2b_ref, gain_ref)]
    pgs = [jnp.concatenate([r[...] for r in pair], axis=0) for pair in (pg_refs[::2], pg_refs[1::2])]
    acc = dot(jnp.concatenate(second, axis=0), jnp.concatenate(pgs, axis=1), TN)
    acc_refs[0][...], acc_refs[1][...] = acc[:, :PART], acc[:, PART:]
    for i, scale_ref in enumerate((s1a_ref, s1b_ref)):
        first = gained(x1_ref[R * i : R * i + R], scale_ref, gain_ref)
        turned_ref[:, columns(i)] = jnp.transpose(first)


def last_weight_kernel(acc0_ref, acc1_ref, turned_ref, *refs):
    pg_refs, (out_ref, held, sems) = refs[:4], refs[4:]
    pgs = [jnp.concatenate([r[...] for r in pair], axis=0) for pair in (pg_refs[:2], pg_refs[2:])]
    pieces = sems.shape[0]
    size = HALF // pieces
    copies = []
    for i in range(pieces):
        rows = pl.ds(i * size, size)
        for half, acc_ref in enumerate((acc0_ref, acc1_ref)):
            part = (acc_ref[rows] + dot(turned_ref[rows], pgs[half])).astype(BF16)
            place = 0
            for start, width in half_pieces(half):
                held[rows, start : start + width] = part[:, place : place + width]
                place += width
        copies.append(pltpu.make_async_copy(held.at[rows], out_ref.at[rows], sems.at[i]))
        copies[-1].start()
    for copy in copies:
        copy.wait()


MIB = 1024 * 1024
PARAMS = pltpu.CompilerParams(vmem_limit_bytes=20 * MIB)
FIRST = pltpu.CompilerParams(vmem_limit_bytes=62 * MIB + MIB // 8)


def shape_of(dtype, *shape):
    return jax.ShapeDtypeStruct(shape, dtype)


def block(*shape):
    return pl.BlockSpec(shape, lambda i: (0,) * len(shape))


def call(
    kernel, args, outs, name, specs=None, out_specs=None, scratch=(), params=PARAMS, flops=1
):
    specs = specs or {}
    return pl.pallas_call(
        kernel,
        grid=(1,),
        in_specs=[specs.get(i) or block(*a.shape) for i, a in enumerate(args)],
        out_specs=out_specs or [block(*o.shape) for o in outs],
        out_shape=list(outs),
        scratch_shapes=list(scratch),
        compiler_params=params,
        cost_estimate=pl.CostEstimate(flops=flops, bytes_accessed=1, transcendentals=0),
        name=name,
    )(*args)


def swap(value):
    return lax.ppermute(value, "stretch", [(0, 1), (1, 0)])


def hop(value, step):
    count = lax.axis_size("blk")
    return lax.ppermute(value, "blk", [(i, (i + step) % count) for i in range(count)])


def after(value, *others):
    return lax.optimization_barrier((value, *others))[0]


PARTS = [shape_of(BF16, R, JOINT + 128), shape_of(F32, R, JOINT), shape_of(F32, R, 128)]
IN_HBM = pl.BlockSpec(memory_space=pltpu.HBM)


def project_first(x, w_in, gain):
    return call(
        project_first_kernel, [x, gain, w_in], PARTS[:1] * 2, "project_first", params=FIRST,
        specs={0: IN_HBM, 2: IN_HBM},
        scratch=[
            pltpu.VMEM((T, HALF), BF16), pltpu.VMEM((HALF, JOINT), BF16),
            pltpu.VMEM((T, JOINT), F32), pltpu.SemaphoreType.DMA, pltpu.SemaphoreType.DMA((2,)),
        ],
    )


def project(x, layer):
    w_in, _, gain = layer[:3]
    return call(project_kernel, [x, gain, w_in], PARTS, "project")


def attend(stream, turn, x, parts, layer, bias, trig, before, cut=1):
    recv, own, sums = parts
    seen = R * (stream + 1)
    shapes = [
        shape_of(BF16, R, HALF), shape_of(BF16, R, HEADS), shape_of(BF16, R, HEADS),
        shape_of(BF16, R, KEYS), shape_of(BF16, R, KEYS), shape_of(BF16, 8 * seen, T),
        shape_of(F32, R, 128),
    ]
    if turn:
        shapes += [shape_of(F32, R, HEADS)] + [shape_of(BF16, R, HEADS // cut)] * cut
    outs = call(
        partial(attend_kernel, stream, turn),
        [recv, own, sums, x, layer[1], layer[4], bias, *trig, *before], shapes, "attend",
        flops=10**10 if turn and not stream else 1,
    )
    out, att, q, k, v, p, scale = outs[:7]
    kept = dict(x=x, att=att, q=q, kv=[k, v], p=p, scale=scale, out=out)
    if turn:
        kept["own"], kept["msgs"] = outs[7], outs[8:]
    return kept


def back(stream, halves, recvs, own, kept, trig, kv, given=None, layer=None, begun=None):
    taken = dict(recvs, own=own, q=kept["q"], p=kept["p"], cos=trig[0], sin=trig[1])
    taken.update(zip(("ka", "va", "kb", "vb"), kv))
    taken.update(given or {})
    outs = {"pg%d" % half: shape_of(BF16, R, PART) for half in halves}
    if stream:
        outs.update({n + str(h): shape_of(F32, R, KEYS // 2) for n in ("dk", "dv") for h in halves})
    if layer:
        taken["w"] = layer[3]
        if 1 in halves:
            taken.update(x=kept["x"], gain=layer[2], scale=kept["scale"], up=kept["out"])
            taken.update(begun or {})
            outs["out"] = shape_of(BF16, R, HALF)
        else:
            outs.update(total=shape_of(F32, R, 128), grad=shape_of(F32, R, HALF))
    names = [*taken, *outs]
    done = call(
        partial(attend_back_kernel, stream, halves, names), list(taken.values()),
        list(outs.values()), "attend_back",
    )
    return dict(zip(outs, done))


def output_back(up, layer, cut=1):
    return call(
        output_back_kernel, [up, layer[4]],
        [shape_of(F32, R, HEADS)] + [shape_of(BF16, R, HEADS // cut)] * cut, "output_back",
    )


def only(outs, *names):
    return {name: value for name, value in outs.items() if name.startswith(names)}


def shards(activations, document_ids, joint_input_weights, output_weights, norm_gains):
    blk = lax.axis_index("blk")
    w_in, w_out, gain = joint_input_weights[0], output_weights[0], norm_gains
    tables_in = [jnp.asarray(t) for t in tables()]

    x1 = activations
    msg_a, msg_b = project_first(x1, w_in, gain)
    recv_a = swap(msg_a)
    recv_b = swap(msg_b)
    ids, x1, w_in, w_out, _ = lax.optimization_barrier(
        (document_ids, x1, w_in, w_out, msg_b)
    )
    next_blk = lax.rem(blk + 1, lax.axis_size("blk"))
    docs = [
        lax.dynamic_slice_in_dim(ids, i * T, T).astype(F32)[None, :] for i in (blk, next_blk)
    ]
    bias1, bias2, *trig = call(
        prepare_kernel, [*docs, *tables_in],
        [shape_of(F32, T, T)] * 2 + [shape_of(F32, T, 128)] * 2, "prepare",
    )
    x1 = after(x1, bias1)
    own_a, sums_a, own_b, sums_b, w_in_t, w_out_t = call(
        project_own_kernel, [x1, gain, w_in, w_out],
        PARTS[1:] * 2 + [shape_of(BF16, JOINT, HALF), shape_of(BF16, HALF, HEADS)], "project_own",
    )
    layer = (w_in, w_out, gain, w_in_t, w_out_t)
    a1 = attend(0, False, x1, (recv_a, own_a, sums_a), layer, bias1, trig, [])
    xa = hop(a1["out"], -1)
    msg_a, own_a, sums_a = project(xa, layer)
    recv_a = swap(msg_a)
    recv_b = after(recv_b, msg_a)
    b1 = attend(1, False, x1, (recv_b, own_b, sums_b), layer, bias1, trig, a1["kv"])
    xb = hop(b1["out"], -1)
    msg_b, own_b, sums_b = project(after(xb, msg_a), layer)
    recv_b = swap(msg_b)
    a2 = attend(0, True, xa, (recv_a, own_a, sums_a), layer, bias2, trig, [])
    recv_a = swap(a2["msgs"][0])
    b2 = attend(
        1, True, xb, (recv_b, own_b, sums_b), layer, bias2, trig, a2["kv"], cut=2
    )
    begun_out = call(
        early_output_kernel, [a2["att"], b2["att"], a2["out"], b2["out"]],
        [shape_of(F32, HEADS, HALF)], "early_output",
    )[0]
    recvs_b = [swap(msg) for msg in b2["msgs"]]
    recvs_b[0] = after(recvs_b[0], recv_a, begun_out)
    kv = a2["kv"] + b2["kv"]
    first = back(1, (0,), {"recv0": recvs_b[0]}, b2["own"], b2, trig, kv, layer=layer)
    pgb2 = back(
        1, (1,), {"recv1": recvs_b[1]}, b2["own"], b2, trig, kv, layer=layer,
        begun=only(first, "total", "grad"),
    )
    pgb2.update(only(first, "pg", "d"))
    upb = hop(pgb2["out"], 1)
    pga2 = back(
        0, (0, 1), {"recv": recv_a}, a2["own"], a2, trig, a2["kv"], only(pgb2, "d"), layer
    )
    upa = hop(pga2["out"], 1)

    *accs, turned = call(
        early_weight_kernel,
        [
            x1, xa, xb, a1["scale"], b1["scale"], a2["scale"], b2["scale"], gain,
            pga2["pg0"], pga2["pg1"], pgb2["pg0"], pgb2["pg1"],
        ],
        [shape_of(F32, HALF, PART)] * 2 + [shape_of(BF16, HALF, T)], "early_weights",
    )
    own_b, msg_b = output_back(after(upb, turned), layer)
    recv_b = swap(msg_b)
    own_a, *msgs_a = output_back(after(upa, msg_b), layer, 2)
    recvs_a = [swap(msg) for msg in msgs_a]
    (total_out,) = call(
        output_weight_kernel, [a1["att"], b1["att"], upa, upb, begun_out],
        [shape_of(BF16, HEADS, HALF)], "output_weights", out_specs=[IN_HBM],
        scratch=[pltpu.VMEM((HEADS, HALF), BF16), pltpu.SemaphoreType.DMA((8,))],
    )
    pgb1 = back(1, (0, 1), {"recv": recv_b}, own_b, b1, trig, a1["kv"] + b1["kv"])
    pga1 = {}
    for half in range(2):
        pga1.update(
            back(
                0, (half,), {"recv%d" % half: recvs_a[half]}, own_a, a1, trig, a1["kv"],
                only(pgb1, "dk%d" % half, "dv%d" % half),
            )
        )
    (total_in,) = call(
        last_weight_kernel,
        [*accs, turned, pga1["pg0"], pgb1["pg0"], pga1["pg1"], pgb1["pg1"]],
        [shape_of(BF16, HALF, JOINT)], "last_weights", out_specs=[IN_HBM],
        scratch=[pltpu.VMEM((HALF, JOINT), BF16), pltpu.SemaphoreType.DMA((8,))],
    )
    return (total_in[None], total_out[None])


def solution(mesh):
    placed = (
        P("blk", "stretch"),
        P(),
        P("blk", "stretch", None),
        P("blk", None, "stretch"),
        P("blk", "stretch"),
    )
    return jax.shard_map(
        shards,
        mesh=mesh,
        in_specs=placed,
        out_specs=(P("blk", "stretch", None), P("blk", None, "stretch")),
        check_vma=False,
    )
```
